128 devices in a mesh: dp: 8 (over x_lo, y), ctx: 16 (over x_hi, z, core).
Axes of the slice: x: 4 (x_hi: 2, x_lo: 2; x = x_hi * 2 + x_lo), y: 4, z: 4, core: 2. Of those that a mesh axis runs over, the one named last changes fastest.
Arguments:
- query_rows: bfloat16 [8, 2048, 4096], P('dp', 'ctx'), may hold values from -6 to 6
- key_rows: bfloat16 [8, 2048, 4096], P('dp', 'ctx'), may hold values from -6 to 6
- value_rows: bfloat16 [8, 2048, 4096], P('dp', 'ctx'), may hold values from -6 to 6
- grad_out: bfloat16 [8, 2048, 4096], P('dp', 'ctx'), may hold values from -6 to 6
- filter_taps: float32 [2048, 4096], P(None, 'ctx'), may hold values from -1.1 to 1.1
- skip_gain: float32 [4096], P('ctx'), may hold values from -1.5 to 1.5
Outputs:
- grad_query: bfloat16 [8, 2048, 4096], P('dp', 'ctx')
- grad_key: bfloat16 [8, 2048, 4096], P('dp', 'ctx')
- grad_value: bfloat16 [8, 2048, 4096], P('dp', 'ctx')
- grad_filter: float32 [2048, 4096], P('dp', 'ctx')
- grad_skip: float32 [4096], P(('ctx', 'dp'))
The draws below stay inside these ranges and needn't reach their ends.
All inputs are finite; a program needn't handle non-finite values.
Results may differ from the reference program's by a relative error of at most 0.013.
Values may be sent and summed in bfloat16 or wider, within the bound.
A program may use at most 192 MiB of HBM per device.

```python
import math
import jax
import jax.numpy as jnp
from jax import lax

D = 4096
SEQ = 2048
SEQS = 8


def draw_filter_taps(key, part):
    key = jax.random.fold_in(key, 11)
    rate_key, noise_key = jax.random.split(key, 2)
    slowest = math.log(10.0) / SEQ
    fastest = max(2.0 * slowest, 1.0 / 30.0)
    log_rate = jax.random.uniform(rate_key, (1, D), jnp.float32, math.log(slowest), math.log(fastest))
    rates = jnp.exp(log_rate)
    steps = jnp.arange(SEQ, dtype=jnp.float32)[:, None]
    noise = jnp.clip(jax.random.normal(noise_key, (SEQ, D), jnp.float32), -4.0, 4.0)
    return noise * jnp.sqrt(1.0 - jnp.exp(-2.0 * rates)) * jnp.exp(-rates * steps)


def levels(key, dims, cuts, low, high):
    loudness, own = 1.0, jax.random.fold_in(key, 6)
    for position, shards_of in cuts:
        steps = jnp.exp(jax.random.uniform(jax.random.fold_in(own, position), (shards_of,), jnp.float32, low / len(cuts), high / len(cuts)))
        loudness = loudness * jnp.repeat(steps, dims[position] // shards_of).reshape([-1 if axis == position else 1 for axis in range(len(dims))])
    return loudness


def bell_draw(rng, shape, width, bound, pieces=(), held_as=jnp.bfloat16):
    values = jax.random.normal(rng, shape, jnp.float32) * width
    if len(pieces) > 0:
        values = levels(rng, shape, pieces, -0.22, 0.18) * values
    return jnp.clip(values, min=-bound, max=bound).astype(held_as)


def setup_inputs(seed: int = 0) -> dict:
    arg_keys = jax.random.split(jax.random.key(seed), 7)
    query_rows = bell_draw(arg_keys[0], (SEQS, SEQ, D), 1.0, 6.0, ((0, 8), (1, 16)))
    key_rows = bell_draw(arg_keys[1], (SEQS, SEQ, D), 1.0, 6.0, ((0, 8), (1, 16)))
    value_rows = bell_draw(arg_keys[2], (SEQS, SEQ, D), 1.0, 6.0, ((0, 8), (1, 16)))
    grad_out = bell_draw(arg_keys[3], (SEQS, SEQ, D), 1.0, 6.0, ((0, 8), (1, 16)))
    filter_taps = draw_filter_taps(jax.random.fold_in(arg_keys[6], 71), 0)
    skip_gain = jnp.clip(jax.random.uniform(arg_keys[5], (D,), jnp.float32, -1.5, 1.5) * levels(arg_keys[5], (D,), ((0, 16),), -0.4, 0.0), -1.5, 1.5)
    return {"query_rows": query_rows, "key_rows": key_rows, "value_rows": value_rows, "grad_out": grad_out, "filter_taps": filter_taps, "skip_gain": skip_gain}


def one_sequence(query_rows, key_rows, value_rows, grad_out, filter_taps, skip_gain):
    length = filter_taps.shape[0]
    total = 2 * length
    gated = (key_rows.astype(jnp.float32) * value_rows.astype(jnp.float32)).astype(jnp.bfloat16)
    grad_conv = (grad_out.astype(jnp.float32) * query_rows.astype(jnp.float32)).astype(jnp.bfloat16)
    gated_wide = gated.astype(jnp.float32)
    grad_wide = grad_conv.astype(jnp.float32)
    spec_filter = jnp.fft.rfft(filter_taps, n=total, axis=0)
    spec_gated = jnp.fft.rfft(gated_wide, n=total, axis=0)
    spec_grad = jnp.fft.rfft(grad_wide, n=total, axis=0)
    conv_long = jnp.fft.irfft(spec_filter * spec_gated, n=total, axis=0)[:length]
    conv_out = (conv_long + skip_gain[None, :] * gated_wide).astype(jnp.bfloat16)
    back_long = jnp.fft.irfft(jnp.conj(spec_filter) * spec_grad, n=total, axis=0)[:length]
    grad_gated = (back_long + skip_gain[None, :] * grad_wide).astype(jnp.bfloat16)
    filter_part = jnp.fft.irfft(spec_grad * jnp.conj(spec_gated), n=total, axis=0)[:length]
    skip_part = jnp.sum(grad_wide * gated_wide, axis=0)
    grad_query = (grad_out.astype(jnp.float32) * conv_out.astype(jnp.float32)).astype(jnp.bfloat16)
    grad_key = (grad_gated.astype(jnp.float32) * value_rows.astype(jnp.float32)).astype(jnp.bfloat16)
    grad_value = (grad_gated.astype(jnp.float32) * key_rows.astype(jnp.float32)).astype(jnp.bfloat16)
    return grad_query, grad_key, grad_value, filter_part.astype(filter_taps.dtype), skip_part.astype(filter_taps.dtype)


def reference(query_rows, key_rows, value_rows, grad_out, filter_taps, skip_gain):
    def per_sequence(items):
        return one_sequence(items[0], items[1], items[2], items[3], filter_taps, skip_gain)

    grad_query, grad_key, grad_value, filter_parts, skip_parts = lax.map(per_sequence, (query_rows, key_rows, value_rows, grad_out))
    return grad_query, grad_key, grad_value, jnp.sum(filter_parts, axis=0), jnp.sum(skip_parts, axis=0)
```

```python
import functools

import jax
import jax.numpy as jnp
from jax import lax
from jax.experimental import pallas as pl
from jax.experimental.pallas import tpu as pltpu
from jax.sharding import PartitionSpec as P

F32 = jnp.float32
BF16 = jnp.bfloat16
B = 128
LIMIT = 56 * 1024 * 1024


def dot_nn(a, b):
    return lax.dot_general(a, b, (((1,), (0,)), ((), ())), preferred_element_type=F32)


def dot_nt(a, b):
    return lax.dot_general(a, b, (((1,), (1,)), ((), ())), preferred_element_type=F32)


def iotas(shape):
    return (
        lax.broadcasted_iota(jnp.int32, shape, 0),
        lax.broadcasted_iota(jnp.int32, shape, 1),
    )


def one_hot(cond):
    return jnp.where(cond, 1.0, 0.0).astype(BF16)


def product(a, b):
    return (a.astype(F32) * b.astype(F32)).astype(BF16)


def prepare_kernel(share, q_ref, k_ref, v_ref, o_ref, s_ref):
    rows, cols = iotas((256, 256))
    eye = one_hot(rows == cols)
    for m in range(q_ref.shape[1] // 256):
        at = slice(256 * m, 256 * m + 256)
        per = 256 // share
        for which, (a, b) in enumerate(((k_ref, v_ref), (o_ref, q_ref))):
            turned = dot_nt(eye, product(a[:, at], b[:, at])).astype(BF16)
            s_ref[per * m : per * m + per, which * share : which * share + share, :] = (
                turned.reshape(per, share, B)
            )


def prepare(share, q, k, v, o):
    width = q.shape[1]
    step = 1024
    spec = pl.BlockSpec((B, step), lambda i: (0, i))
    return pl.pallas_call(
        functools.partial(prepare_kernel, share),
        grid=(width // step,),
        in_specs=[spec] * 4,
        out_specs=pl.BlockSpec((step // share, 2 * share, B), lambda i: (i, 0, 0)),
        out_shape=jax.ShapeDtypeStruct((width // share, 2 * share, B), BF16),
        name="prepare",
    )(q, k, v, o)


def swap_matrix():
    rows, cols = iotas((256, 256))
    return one_hot(cols == (rows % 16) * 16 + rows // 16)


def convolve_kernel(
    share, r_ref, f_ref, skip_ref, s_ref, g_ref, taps, xs, gs, ys, zs, x2, g2, t_rows, t_cols
):
    lags = f_ref.shape[0]
    blocks = lags // B
    first = lax.axis_index("dp") * share
    rows, cols = iotas((share, f_ref.shape[1]))
    pick = one_hot(cols == rows + first)
    for m in range(lags // 256):
        at = slice(256 * m, 256 * m + 256)
        taps[:, :, at] = dot_nt(pick, f_ref[at, :].astype(BF16)).reshape(share, 1, 256)
    swap = swap_matrix()

    xs[:, 0:8, :] = jnp.zeros((share, 8, B), F32)
    gs[:, B : B + 8, :] = jnp.zeros((share, 8, B), F32)

    @pl.loop(0, 8)
    def _(i):
        at = pl.multiple_of(i * 16, 16)
        for half in range(share // 16):
            for which in range(2):
                block = r_ref[pl.ds(at, 16), which * share + half * 16 : which * share + half * 16 + 16, :]
                out = dot_nn(swap, block.reshape(256, B)).reshape(16, 16, B)
                if which == 0:
                    xs[half * 16 : half * 16 + 16, pl.ds(at + 8, 16), :] = out
                else:
                    gs[half * 16 : half * 16 + 16, pl.ds(at, 16), :] = out

    x2[0:B, :] = jnp.zeros((B, 2 * B), BF16)
    g2[B : 2 * B, :] = jnp.zeros((B, 2 * B), BF16)
    rows, cols = iotas((B, B))
    flip = one_hot(rows + cols == B - 1)

    @pl.loop(0, share)
    def _(d):
        x = xs[d, 8 : B + 8, :]
        x2[B : 2 * B, 0:B] = x.astype(BF16)
        x2[B : 2 * B, B : 2 * B] = xs[d, 0:B, :].astype(BF16)
        g = gs[d, 0:B, :]
        g2[0:B, 0:B] = g.astype(BF16)
        g2[0:B, B : 2 * B] = gs[d, 8 : B + 8, :].astype(BF16)
        rows, cols = iotas((B, B))
        low = cols >= rows
        before = jnp.zeros((B, B), F32)
        for k in range(blocks):
            line = taps[d, :, B * k : B * k + B]
            turned = pltpu.roll(jnp.broadcast_to(line, (B, B)), 0, 1, stride=1, stride_axis=0)
            t = jnp.where(low, turned, before).astype(BF16)
            t_rows[B * k : B * k + B, :] = t
            t_cols[:, B * k : B * k + B] = t
            before = turned
        gain = skip_ref[first + d]
        y = gain * x
        z = gain * g
        for j in range(blocks // 2):
            y = y + dot_nn(x2[B - 16 * j : 2 * B - 16 * j, :], t_rows[256 * j : 256 * j + 256, :])
            z = z + dot_nt(g2[16 * j : 16 * j + B, :], t_cols[:, 256 * j : 256 * j + 256])
        ys[d] = y.astype(BF16)
        zs[d] = z.astype(BF16)
        x_turned = dot_nt(flip, x2[B : 2 * B, 0:B]).astype(BF16)
        keep = cols + rows >= B - 1
        after = jnp.zeros((B, B), F32)
        for j in reversed(range(blocks // 2)):
            pair = dot_nn(x_turned, g2[16 * j : 16 * j + B, :])
            for k, part in ((2 * j + 1, pair[:, B:]), (2 * j, pair[:, :B])):
                mixed = jnp.where(keep, part, after)
                turned = pltpu.roll(mixed, 1, 1, stride=1, stride_axis=0)
                g_ref[d, :, B * k : B * k + B] = jnp.sum(turned, axis=0, keepdims=True)
                after = part

    @pl.loop(0, 8)
    def _(i):
        at = pl.multiple_of(i * 16, 16)
        for half in range(share // 16):
            for which, ref in enumerate((ys, zs)):
                block = ref[half * 16 : half * 16 + 16, pl.ds(at, 16), :]
                out = dot_nn(swap, block.reshape(256, B)).astype(BF16).reshape(16, 16, B)
                s_ref[pl.ds(at, 16), which * share + half * 16 : which * share + half * 16 + 16, :] = out


def convolve(share, received, filter_taps, skip_gain):
    lags = filter_taps.shape[0]
    vmem = pl.BlockSpec(memory_space=pltpu.VMEM)
    return pl.pallas_call(
        functools.partial(convolve_kernel, share),
        in_specs=[vmem, vmem, pl.BlockSpec(memory_space=pltpu.SMEM)],
        out_specs=[vmem, vmem],
        out_shape=[
            jax.ShapeDtypeStruct(received.shape, BF16),
            jax.ShapeDtypeStruct((share, 1, lags), F32),
        ],
        scratch_shapes=[
            pltpu.VMEM((share, 1, lags), F32),
            pltpu.VMEM((share, B + 8, B), F32),
            pltpu.VMEM((share, B + 8, B), F32),
            pltpu.VMEM((share, B, B), BF16),
            pltpu.VMEM((share, B, B), BF16),
            pltpu.VMEM((2 * B, 2 * B), BF16),
            pltpu.VMEM((2 * B, 2 * B), BF16),
            pltpu.VMEM((lags, B), BF16),
            pltpu.VMEM((B, lags), BF16),
        ],
        compiler_params=pltpu.CompilerParams(vmem_limit_bytes=LIMIT),
        name="convolve",
    )(received, filter_taps, skip_gain)


def finish_kernel(share, r_ref, k_ref, v_ref, o_ref, dq_ref, dk_ref, dv_ref):
    rows, cols = iotas((B, B))
    eye = one_hot(rows == cols)
    per = 256 // share
    for m in range(k_ref.shape[1] // 256):
        at = slice(256 * m, 256 * m + 256)
        conv, back = (
            dot_nt(
                eye,
                r_ref[per * m : per * m + per, which * share : which * share + share, :].reshape(256, B),
            )
            for which in range(2)
        )
        dq_ref[:, at] = (o_ref[:, at].astype(F32) * conv).astype(BF16)
        dk_ref[:, at] = (v_ref[:, at].astype(F32) * back).astype(BF16)
        dv_ref[:, at] = (k_ref[:, at].astype(F32) * back).astype(BF16)


def finish(share, received, k, v, o):
    width = k.shape[1]
    step = 1024
    spec = pl.BlockSpec((B, step), lambda i: (0, i))
    return pl.pallas_call(
        functools.partial(finish_kernel, share),
        grid=(width // step,),
        in_specs=[pl.BlockSpec((step // share, 2 * share, B), lambda i: (i, 0, 0))] + [spec] * 3,
        out_specs=[spec] * 3,
        out_shape=[jax.ShapeDtypeStruct((B, width), BF16)] * 3,
        name="finish",
    )(received, k, v, o)


def per_device(query_rows, key_rows, value_rows, grad_out, filter_taps, skip_gain):
    q, k, v, o = query_rows[0], key_rows[0], value_rows[0], grad_out[0]
    share = q.shape[1] // (lax.axis_size("ctx") * lax.axis_size("dp"))
    every = ("ctx", "dp")
    sent = prepare(share, q, k, v, o)
    received = lax.all_to_all(sent, every, split_axis=0, concat_axis=0, tiled=True)
    back, filter_rows = convolve(share, received, filter_taps, skip_gain)
    filter_rows = filter_rows[:, 0, :]
    returned = lax.all_to_all(back, every, split_axis=0, concat_axis=0, tiled=True)
    dq, dk, dv = finish(share, returned, k, v, o)
    filter_part = lax.all_to_all(filter_rows, "dp", split_axis=1, concat_axis=0, tiled=True)
    return dq[None], dk[None], dv[None], jnp.transpose(filter_part), filter_rows[:, 0]


def solution(mesh):
    rows = P("dp", "ctx", None)
    return jax.shard_map(
        per_device,
        mesh=mesh,
        in_specs=(rows, rows, rows, rows, P(None, "ctx"), P("ctx")),
        out_specs=(rows, rows, rows, P("dp", "ctx"), P(("ctx", "dp"))),
        check_vma=False,
    )
```

```python
import functools

import jax
import jax.numpy as jnp
from jax import lax
from jax.experimental import pallas as pl
from jax.experimental.pallas import tpu as pltpu
from jax.sharding import PartitionSpec as P

F32 = jnp.float32
BF16 = jnp.bfloat16
B = 128
LIMIT = 56 * 1024 * 1024


def dot_nn(a, b):
    return lax.dot_general(a, b, (((1,), (0,)), ((), ())), preferred_element_type=F32)


def dot_nt(a, b):
    return lax.dot_general(a, b, (((1,), (1,)), ((), ())), preferred_element_type=F32)


def iotas(shape):
    return (
        lax.broadcasted_iota(jnp.int32, shape, 0),
        lax.broadcasted_iota(jnp.int32, shape, 1),
    )


def one_hot(cond):
    return jnp.where(cond, 1.0, 0.0).astype(BF16)


def product(a, b):
    return (a.astype(F32) * b.astype(F32)).astype(BF16)


UNITS = 4
UNIT = 8
BLOCK = 2 * UNIT
MESH = pl.DeviceIdType.MESH


def prepare_kernel(q_ref, k_ref, v_ref, o_ref, s_ref):
    rows, cols = iotas((256, 256))
    place = one_hot(
        cols == (rows // 8 % 2) * 128 + (rows // 64) * 32 + (rows // 16 % 4) * 8 + rows % 8
    )
    for m in range(q_ref.shape[1] // 256):
        for half in range(2):
            at = slice(256 * m + 128 * half, 256 * m + 128 * half + 128)
            both = jnp.concatenate(
                [product(k_ref[:, at], v_ref[:, at]), product(o_ref[:, at], q_ref[:, at])], axis=1
            )
            turned = dot_nt(place, both).astype(BF16).reshape(4, UNITS, BLOCK, B)
            for u in range(UNITS):
                s_ref[u, 4 * half : 4 * half + 4, m] = turned[:, u]


def prepare(q, k, v, o):
    step = 1024
    spec = pl.BlockSpec((B, step), lambda i: (0, i))
    return pl.pallas_call(
        prepare_kernel,
        grid=(q.shape[1] // step,),
        in_specs=[spec] * 4,
        out_specs=pl.BlockSpec((UNITS, 8, 4, BLOCK, B), lambda i: (0, i // 2, i % 2, 0, 0)),
        out_shape=jax.ShapeDtypeStruct((UNITS, 16, 8, BLOCK, B), BF16),
        name="prepare",
    )(q, k, v, o)


def exchange_kernel(
    s_ref, f_ref, skip_ref, r_ref, h_ref, first_ref,
    mid_in, whole_in, out, mid_out, g_out, taps, xs, gs, ys, zs, gu, x2, g2, t_rows, t_cols, swap, flip,
    send, recv, g_send, g_recv, own,
):
    lags = f_ref.shape[0]
    blocks = lags // B
    ctx, dp = lax.axis_index("ctx"), lax.axis_index("dp")
    x_high, zc = ctx // 8, ctx % 8
    plane = x_high * 8 + dp
    x, y, z, core = x_high * 2 + dp // 4, dp % 4, zc // 2, zc % 2

    def plane_peer(n):
        there_x, there_y = (x + n % 4) % 4, (y + n // 4) % 4
        there_dp = (there_x % 2) * 4 + there_y
        device = {"ctx": (there_x // 2) * 8 + zc, "dp": there_dp}
        return device, (there_x // 2) * 8 + there_dp

    def line_peer(n):
        there = ((z + n % 4) % 4) * 2 + (core + n // 4) % 2
        return {"ctx": x_high * 8 + there, "dp": dp}, there

    barrier = pltpu.get_barrier_semaphore()

    @pl.loop(1, 16)
    def _(n):
        pl.semaphore_signal(barrier, 1, device_id=plane_peer(n)[0], device_id_type=MESH)

    @pl.loop(1, 8)
    def _(n):
        pl.semaphore_signal(barrier, 1, device_id=line_peer(n)[0], device_id_type=MESH)

    pl.semaphore_wait(barrier, 22)

    def send_all(phase, u, count, peer, source, target, mine):
        pltpu.make_async_copy(source(mine), target, own.at[phase, u]).start()

        @pl.loop(1, count)
        def _(n):
            device, index = peer(n)
            pltpu.make_async_remote_copy(
                src_ref=source(index),
                dst_ref=target,
                send_sem=send.at[phase, u],
                recv_sem=recv.at[phase, u],
                device_id=device,
                device_id_type=MESH,
            ).start()

    def arrived(phase, u, where, mine, count):
        pltpu.make_async_copy(where.at[u, mine], where.at[u, mine], own.at[phase, u]).wait()
        some = where.at[u, pl.ds(0, count - 1)]
        pltpu.make_async_copy(some, some, recv.at[phase, u]).wait()

    def in_first(u):
        send_all(0, u, 16, plane_peer, lambda i: s_ref.at[u, i], mid_in.at[u, plane], plane)

    def in_second(u):
        arrived(0, u, mid_in, plane, 16)
        send_all(1, u, 8, line_peer, lambda i: mid_in.at[u, :, i], whole_in.at[u, zc], zc)

    def out_first(u):
        send_all(2, u, 8, line_peer, lambda i: out.at[u, i], mid_out.at[u, zc], zc)

    def out_second(u):
        arrived(2, u, mid_out, zc, 8)
        send_all(3, u, 16, plane_peer, lambda i: mid_out.at[u, :, i], r_ref.at[u, plane], plane)

    for u in range(UNITS):
        in_first(u)

    share = UNITS * UNIT
    first = dp * share
    rows, cols = iotas((share, f_ref.shape[1]))
    pick = one_hot(cols == rows + first)
    for m in range(lags // 256):
        at = slice(256 * m, 256 * m + 256)
        taps[:, :, at] = dot_nt(pick, f_ref[at, :].astype(BF16)).reshape(share, 1, 256)
    rows, cols = iotas((256, 256))
    swap[...] = one_hot(cols == (rows % 16) * 16 + rows // 16)
    rows, cols = iotas((B, B))
    flip[...] = one_hot(rows + cols == B - 1)
    xs[:, 0:8, :] = jnp.zeros((UNIT, 8, B), F32)
    gs[:, B : B + 8, :] = jnp.zeros((UNIT, 8, B), F32)
    x2[0:B, :] = jnp.zeros((B, 2 * B), BF16)
    g2[B : 2 * B, :] = jnp.zeros((B, 2 * B), BF16)

    in_second(0)
    in_second(1)

    def unpack(u):
        @pl.loop(0, 8)
        def _(i):
            rows = dot_nn(swap[...], whole_in[u, i].reshape(256, B)).reshape(2, UNIT, 2, 8, B)
            at = pl.multiple_of(i * 8, 8)
            for high in range(2):
                xs[:, pl.ds(at + 64 * high + 8, 8), :] = rows[0, :, high]
                gs[:, pl.ds(at + 64 * high, 8), :] = rows[1, :, high]

    def pack(u):
        @pl.loop(0, 8)
        def _(i):
            at = pl.multiple_of(i * 8, 8)
            parts = [
                jnp.concatenate([ref[:, pl.ds(at, 8), :], ref[:, pl.ds(at + 64, 8), :]], axis=1)
                for ref in (ys, zs)
            ]
            rows = jnp.concatenate(parts, axis=0).astype(BF16).reshape(256, B)
            out[u, i] = dot_nn(swap[...], rows).astype(BF16).reshape(16, BLOCK, B)

        at = pl.multiple_of(u * UNIT, UNIT)
        filter_rows = gu[...].reshape(UNIT, lags)
        for i in range(8):
            g_out[i, pl.ds(at, UNIT), :] = filter_rows[:, 256 * i : 256 * i + 256]

    def channel(u, d):
        x = xs[d, 8 : B + 8, :]
        x2[B : 2 * B, 0:B] = x.astype(BF16)
        x2[B : 2 * B, B : 2 * B] = xs[d, 0:B, :].astype(BF16)
        g = gs[d, 0:B, :]
        g2[0:B, 0:B] = g.astype(BF16)
        g2[0:B, B : 2 * B] = gs[d, 8 : B + 8, :].astype(BF16)
        rows, cols = iotas((B, B))
        low = cols >= rows
        before = jnp.zeros((B, B), F32)
        for k in range(blocks):
            line = taps[u * UNIT + d, :, B * k : B * k + B]
            turned = pltpu.roll(jnp.broadcast_to(line, (B, B)), 0, 1, stride=1, stride_axis=0)
            t = jnp.where(low, turned, before).astype(BF16)
            t_rows[B * k : B * k + B, :] = t
            t_cols[:, B * k : B * k + B] = t
            before = turned
        gain = skip_ref[first + u * UNIT + d]
        y = gain * x
        z = gain * g
        for j in range(blocks // 2):
            y = y + dot_nn(x2[B - 16 * j : 2 * B - 16 * j, :], t_rows[256 * j : 256 * j + 256, :])
            z = z + dot_nt(g2[16 * j : 16 * j + B, :], t_cols[:, 256 * j : 256 * j + 256])
        ys[d] = y
        zs[d] = z
        x_turned = dot_nt(flip[...], x2[B : 2 * B, 0:B]).astype(BF16)
        keep = cols + rows >= B - 1
        after = jnp.zeros((B, B), F32)
        for j in reversed(range(blocks // 2)):
            pair = dot_nn(x_turned, g2[16 * j : 16 * j + B, :])
            for k, part in ((2 * j + 1, pair[:, B:]), (2 * j, pair[:, :B])):
                mixed = jnp.where(keep, part, after)
                turned = pltpu.roll(mixed, 1, 1, stride=1, stride_axis=0)
                gu[d, :, B * k : B * k + B] = jnp.sum(turned, axis=0, keepdims=True)
                after = part

    @pl.loop(0, 2 * UNITS)
    def _(step):
        u, half = step // 2, step % 2

        @pl.when(half == 0)
        def _():
            arrived(1, u, whole_in, zc, 8)
            unpack(u)

        @pl.loop(0, UNIT // 2)
        def _(d):
            channel(u, half * (UNIT // 2) + d)

        @pl.when(jnp.logical_and(half == 0, u < UNITS - 2))
        def _():
            in_second(u + 2)

        @pl.when(jnp.logical_and(half == 0, u > 0))
        def _():
            out_second(u - 1)

        @pl.when(half == 1)
        def _():
            pack(u)
            out_first(u)

    def g_copy(n):
        there = (dp + n) % 8
        return pltpu.make_async_remote_copy(
            src_ref=g_out.at[there],
            dst_ref=h_ref.at[dp],
            send_sem=g_send,
            recv_sem=g_recv,
            device_id={"ctx": ctx, "dp": there},
            device_id_type=MESH,
        )

    own_g = pltpu.make_async_copy(g_out.at[dp], h_ref.at[dp], own.at[4, 0])
    own_g.start()

    @pl.loop(1, 8)
    def _(n):
        g_copy(n).start()

    first_ref[...] = g_out[0, :, 0:B]
    out_second(UNITS - 1)
    for u in range(UNITS):
        arrived(3, u, r_ref, plane, 16)
    own_g.wait()
    for sem in (g_recv, g_send):
        pltpu.make_async_copy(h_ref.at[pl.ds(0, 7)], h_ref.at[pl.ds(0, 7)], sem).wait()
    for u in range(UNITS):
        for phase, some in ((0, mid_in.at[u, 0:15]), (1, whole_in.at[u, 0:7]), (2, mid_out.at[u, 0:7]), (3, r_ref.at[u, 0:15])):
            pltpu.make_async_copy(some, some, send.at[phase, u]).wait()


def exchange(sent, filter_taps, skip_gain):
    lags = filter_taps.shape[0]
    share = UNITS * UNIT
    vmem = pl.BlockSpec(memory_space=pltpu.VMEM)
    anywhere = pl.BlockSpec(memory_space=pl.ANY)
    return pl.pallas_call(
        exchange_kernel,
        in_specs=[anywhere, vmem, pl.BlockSpec(memory_space=pltpu.SMEM)],
        out_specs=[anywhere, anywhere, vmem],
        out_shape=[
            jax.ShapeDtypeStruct((UNITS, 16, 8, BLOCK, B), BF16),
            jax.ShapeDtypeStruct((8, share, lags // 8), F32),
            jax.ShapeDtypeStruct((share, B), F32),
        ],
        scratch_shapes=[
            pltpu.VMEM((UNITS, 16, 8, BLOCK, B), BF16),
            pltpu.VMEM((UNITS, 8, 16, BLOCK, B), BF16),
            pltpu.VMEM((UNITS, 8, 16, BLOCK, B), BF16),
            pltpu.VMEM((UNITS, 8, 16, BLOCK, B), BF16),
            pltpu.VMEM((8, share, lags // 8), F32),
            pltpu.VMEM((share, 1, lags), F32),
            pltpu.VMEM((UNIT, B + 8, B), F32),
            pltpu.VMEM((UNIT, B + 8, B), F32),
            pltpu.VMEM((UNIT, B, B), F32),
            pltpu.VMEM((UNIT, B, B), F32),
            pltpu.VMEM((UNIT, 1, lags), F32),
            pltpu.VMEM((2 * B, 2 * B), BF16),
            pltpu.VMEM((2 * B, 2 * B), BF16),
            pltpu.VMEM((lags, B), BF16),
            pltpu.VMEM((B, lags), BF16),
            pltpu.VMEM((256, 256), BF16),
            pltpu.VMEM((B, B), BF16),
            pltpu.SemaphoreType.DMA((4, UNITS)),
            pltpu.SemaphoreType.DMA((4, UNITS)),
            pltpu.SemaphoreType.DMA,
            pltpu.SemaphoreType.DMA,
            pltpu.SemaphoreType.DMA((5, UNITS)),
        ],
        compiler_params=pltpu.CompilerParams(
            collective_id=0, has_side_effects=True, vmem_limit_bytes=LIMIT
        ),
        name="exchange",
    )(sent, filter_taps, skip_gain)


def finish_kernel(r_ref, k_ref, v_ref, o_ref, dq_ref, dk_ref, dv_ref):
    rows, cols = iotas((256, 256))
    place = one_hot(
        cols == (rows // 8 % 4) * 64 + (rows // 32 % 4) * 16 + (rows // 128) * 8 + rows % 8
    )
    rows, cols = iotas((B, B))
    eye = one_hot(rows == cols)
    for m in range(k_ref.shape[1] // 256):
        for half in range(2):
            at = slice(256 * m + 128 * half, 256 * m + 128 * half + 128)
            mixed = r_ref[:, 4 * half : 4 * half + 4, m].reshape(256, B)
            both = dot_nt(eye, dot_nn(place, mixed).astype(BF16))
            conv, back = both[:, :B], both[:, B:]
            dq_ref[:, at] = (o_ref[:, at].astype(F32) * conv).astype(BF16)
            dk_ref[:, at] = (v_ref[:, at].astype(F32) * back).astype(BF16)
            dv_ref[:, at] = (k_ref[:, at].astype(F32) * back).astype(BF16)


def finish(received, k, v, o):
    width = k.shape[1]
    step = 1024
    spec = pl.BlockSpec((B, step), lambda i: (0, i))
    return pl.pallas_call(
        finish_kernel,
        grid=(width // step,),
        in_specs=[pl.BlockSpec((UNITS, 8, 4, BLOCK, B), lambda i: (0, i // 2, i % 2, 0, 0))] + [spec] * 3,
        out_specs=[spec] * 3,
        out_shape=[jax.ShapeDtypeStruct((B, width), BF16)] * 3,
        name="finish",
    )(received, k, v, o)


def per_device(query_rows, key_rows, value_rows, grad_out, filter_taps, skip_gain):
    q, k, v, o = query_rows[0], key_rows[0], value_rows[0], grad_out[0]
    sent = prepare(q, k, v, o)
    returned, filter_rows, first_lags = exchange(sent, filter_taps, skip_gain)
    dq, dk, dv = finish(returned, k, v, o)
    filter_part = jnp.transpose(filter_rows.reshape(-1, filter_rows.shape[2]))
    return dq[None], dk[None], dv[None], filter_part, first_lags[:, 0]


def solution(mesh):
    rows = P("dp", "ctx", None)
    return jax.shard_map(
        per_device,
        mesh=mesh,
        in_specs=(rows, rows, rows, rows, P(None, "ctx"), P("ctx")),
        out_specs=(rows, rows, rows, P("dp", "ctx"), P(("ctx", "dp"))),
        check_vma=False,
    )
```

```python
import functools

import jax
import jax.numpy as jnp
from jax import lax
from jax.experimental import pallas as pl
from jax.experimental.pallas import tpu as pltpu
from jax.sharding import PartitionSpec as P

F32 = jnp.float32
BF16 = jnp.bfloat16
B = 128
LIMIT = 56 * 1024 * 1024


def dot_nn(a, b):
    return lax.dot_general(a, b, (((1,), (0,)), ((), ())), preferred_element_type=F32)


def dot_nt(a, b):
    return lax.dot_general(a, b, (((1,), (1,)), ((), ())), preferred_element_type=F32)


def iotas(shape):
    return (
        lax.broadcasted_iota(jnp.int32, shape, 0),
        lax.broadcasted_iota(jnp.int32, shape, 1),
    )


def one_hot(cond):
    return jnp.where(cond, 1.0, 0.0).astype(BF16)


def product(a, b):
    return (a.astype(F32) * b.astype(F32)).astype(BF16)


UNITS = 4
UNIT = 8
BLOCK = 2 * UNIT
CHIPS = 64
MESH = pl.DeviceIdType.MESH


def prepare_kernel(q_ref, k_ref, v_ref, o_ref, s_ref):
    rows, cols = iotas((256, 256))
    place = one_hot(
        cols == (rows // 8 % 2) * 128 + (rows // 64) * 32 + (rows // 16 % 4) * 8 + rows % 8
    )
    for m in range(q_ref.shape[1] // 256):
        for half in range(2):
            at = slice(256 * m + 128 * half, 256 * m + 128 * half + 128)
            both = jnp.concatenate(
                [product(k_ref[:, at], v_ref[:, at]), product(o_ref[:, at], q_ref[:, at])], axis=1
            )
            turned = dot_nt(place, both).astype(BF16).reshape(4, UNITS, BLOCK, B)
            for u in range(UNITS):
                s_ref[u, m % 2, half, :, m // 2] = turned[:, u]


def prepare(q, k, v, o):
    step = 2048
    spec = pl.BlockSpec((B, step), lambda i: (0, i))
    return pl.pallas_call(
        prepare_kernel,
        grid=(q.shape[1] // step,),
        in_specs=[spec] * 4,
        out_specs=pl.BlockSpec(
            (UNITS, 2, 2, 4, step // 512, BLOCK, B),
            lambda i: (0, 0, i * step // 2048, 0, i % (2048 // step), 0, 0),
        ),
        out_shape=jax.ShapeDtypeStruct((UNITS, 2, 4, 4, 4, BLOCK, B), BF16),
        name="prepare",
    )(q, k, v, o)


def exchange_kernel(
    s_ref, f_any, skip_ref, r_ref, h_ref, first_ref,
    f_ref, going, come, staged, leaving,
    g_out, taps, xs, gs, ys, zs, gu, x2s, g2s, t_rows_s, t_cols_s, swap, flip,
    own_sems, hand_send, hand_recv, send, recv, stay, g_send, g_recv, g_own, f_sem,
):
    lags = f_ref.shape[0]
    blocks = lags // B
    ctx, dp = lax.axis_index("ctx"), lax.axis_index("dp")
    core = ctx % 2
    x, y, z = (ctx // 8) * 2 + dp // 4, dp % 4, (ctx // 2) % 4
    chip = x * 16 + y * 4 + z
    mate = {"ctx": ctx + 1 - 2 * core, "dp": dp}

    def peer(n):
        m = (n * 27) % CHIPS
        x_there, y_there, z_there = (x + m // 16) % 4, (y + m // 4) % 4, (z + m) % 4
        device = {
            "ctx": (x_there // 2) * 8 + z_there * 2 + core,
            "dp": (x_there % 2) * 4 + y_there,
        }
        return device, x_there * 16 + y_there * 4 + z_there

    def remote(source, target, sems, device):
        pltpu.make_async_remote_copy(
            src_ref=source,
            dst_ref=target,
            send_sem=sems[0],
            recv_sem=sems[1],
            device_id=device,
            device_id_type=MESH,
        ).start()

    def wait_for(some, sem):
        pltpu.make_async_copy(some, some, sem).wait()

    barrier = pltpu.get_barrier_semaphore()
    pl.semaphore_signal(barrier, 1, device_id=mate, device_id_type=MESH)

    @pl.loop(1, CHIPS)
    def _(n):
        pl.semaphore_signal(barrier, 1, device_id=peer(n)[0], device_id_type=MESH)

    def own_copy(u):
        return pltpu.make_async_copy(s_ref.at[u, core], going.at[u, :, core], own_sems.at[u])

    filter_copy = pltpu.make_async_copy(f_any, f_ref, f_sem)
    for u in range(UNITS):
        own_copy(u).start()
    filter_copy.start()
    pl.semaphore_wait(barrier, CHIPS)
    for u in range(UNITS):
        remote(s_ref.at[u, 1 - core], going.at[u, :, core], (hand_send.at[0, u], hand_recv.at[0, u]), mate)

    def spread(way, u, source, target):
        @pl.loop(1, CHIPS)
        def _(n):
            device, there = peer(n)
            remote(source.at[u, there], target.at[u, chip], (send.at[way, u], recv.at[way, u]), device)

        pltpu.make_async_copy(source.at[u, chip], target.at[u, chip], stay.at[way, u]).start()

    def gathered(way, u, target):
        wait_for(target.at[u, chip], stay.at[way, u])
        wait_for(target.at[u, 0 : CHIPS - 1], recv.at[way, u])

    @pl.loop(0, UNITS)
    def _(u):
        own_copy(u).wait()
        wait_for(going.at[u, :, 1 - core], hand_recv.at[0, u])
        spread(0, u, going, come)

    share = UNITS * UNIT
    first = dp * share
    filter_copy.wait()
    rows, cols = iotas((share, f_ref.shape[1]))
    pick = one_hot(cols == rows + first)
    for m in range(lags // 256):
        at = slice(256 * m, 256 * m + 256)
        taps[:, :, at] = dot_nt(pick, f_ref[at, :].astype(BF16)).reshape(share, 1, 256)
    rows, cols = iotas((256, 256))
    swap[...] = one_hot(cols == (rows % 16) * 16 + rows // 16)
    rows, cols = iotas((B, B))
    flip[...] = one_hot(rows + cols == B - 1)
    xs[:, 0:8, :] = jnp.zeros((UNIT, 8, B), F32)
    gs[:, B : B + 8, :] = jnp.zeros((UNIT, 8, B), F32)
    x2s[:, 0:B, :] = jnp.zeros((2, B, 2 * B), BF16)
    g2s[:, B : 2 * B, :] = jnp.zeros((2, B, 2 * B), BF16)

    def unpack(u):
        @pl.loop(0, 4)
        def _(iz):
            for ic in range(2):
                block = jnp.concatenate(
                    [come[u, pl.ds(4 * i + iz, 1), ic] for i in range(16)], axis=0
                ).reshape(256, B)
                rows = dot_nn(swap[...], block).reshape(2, UNIT, 2, 8, B)
                at = pl.multiple_of((iz * 2 + ic) * 8, 8)
                for high in range(2):
                    xs[:, pl.ds(at + 64 * high + 8, 8), :] = rows[0, :, high]
                    gs[:, pl.ds(at + 64 * high, 8), :] = rows[1, :, high]

    def pack(u):
        @pl.loop(0, 4)
        def _(iz):
            for ic in range(2):
                at = pl.multiple_of((iz * 2 + ic) * 8, 8)
                parts = [
                    jnp.concatenate([ref[:, pl.ds(at, 8), :], ref[:, pl.ds(at + 64, 8), :]], axis=1)
                    for ref in (ys, zs)
                ]
                rows = jnp.concatenate(parts, axis=0).astype(BF16).reshape(256, B)
                turned = dot_nn(swap[...], rows).astype(BF16).reshape(16, BLOCK, B)

                @pl.when(core == ic)
                def _():
                    for i in range(16):
                        leaving[u, 4 * i + iz, ic] = turned[i]

                @pl.when(core != ic)
                def _():
                    for i in range(16):
                        staged[u, 4 * i + iz] = turned[i]

        at = pl.multiple_of(u * UNIT, UNIT)
        filter_rows = gu[...].reshape(UNIT, lags)
        for i in range(8):
            g_out[i, pl.ds(at, UNIT), :] = filter_rows[:, 256 * i : 256 * i + 256]

    def send_filter(u):
        at = pl.multiple_of(u * UNIT, UNIT)
        rows = pl.ds(at, UNIT)
        pltpu.make_async_copy(g_out.at[dp, rows], h_ref.at[dp, rows], g_own.at[u]).start()

        @pl.loop(1, 8)
        def _(n):
            there = (dp + n) % 8
            remote(
                g_out.at[there, rows],
                h_ref.at[dp, rows],
                (g_send.at[u], g_recv.at[u]),
                {"ctx": ctx, "dp": there},
            )

    def hand_out(u):
        remote(staged.at[u], leaving.at[u, :, core], (hand_send.at[1, u], hand_recv.at[1, u]), mate)

    def send_out(u):
        wait_for(leaving.at[u, :, 1 - core], hand_recv.at[1, u])
        spread(1, u, leaving, r_ref)

    def channel(u, d, way):
        x2, g2, t_rows, t_cols = x2s.at[way], g2s.at[way], t_rows_s.at[way], t_cols_s.at[way]
        x = xs[d, 8 : B + 8, :]
        x2[B : 2 * B, 0:B] = x.astype(BF16)
        x2[B : 2 * B, B : 2 * B] = xs[d, 0:B, :].astype(BF16)
        g = gs[d, 0:B, :]
        g2[0:B, 0:B] = g.astype(BF16)
        g2[0:B, B : 2 * B] = gs[d, 8 : B + 8, :].astype(BF16)
        rows, cols = iotas((B, B))
        low = cols >= rows
        before = jnp.zeros((B, B), F32)
        for k in range(blocks):
            line = taps[u * UNIT + d, :, B * k : B * k + B]
            turned = pltpu.roll(jnp.broadcast_to(line, (B, B)), 0, 1, stride=1, stride_axis=0)
            t = jnp.where(low, turned, before).astype(BF16)
            t_rows[B * k : B * k + B, :] = t
            t_cols[:, B * k : B * k + B] = t
            before = turned
        gain = skip_ref[first + u * UNIT + d]
        y = gain * x
        z = gain * g
        for j in range(blocks // 2):
            y = y + dot_nn(x2[B - 16 * j : 2 * B - 16 * j, :], t_rows[256 * j : 256 * j + 256, :])
            z = z + dot_nt(g2[16 * j : 16 * j + B, :], t_cols[:, 256 * j : 256 * j + 256])
        ys[d] = y
        zs[d] = z
        x_turned = dot_nt(flip[...], x2[B : 2 * B, 0:B]).astype(BF16)
        keep = cols + rows >= B - 1
        after = jnp.zeros((B, B), F32)
        for j in reversed(range(blocks // 2)):
            pair = dot_nn(x_turned, g2[16 * j : 16 * j + B, :])
            for k, part in ((2 * j + 1, pair[:, B:]), (2 * j, pair[:, :B])):
                mixed = jnp.where(keep, part, after)
                turned = pltpu.roll(mixed, 1, 1, stride=1, stride_axis=0)
                gu[d, :, B * k : B * k + B] = jnp.sum(turned, axis=0, keepdims=True)
                after = part

    @pl.loop(0, 4 * UNITS)
    def _(step):
        u, part = step // 4, step % 4

        @pl.when(part == 0)
        def _():
            gathered(0, u, come)
            unpack(u)

        for d in range(2):
            channel(u, part * 2 + d, d)

        @pl.when(jnp.logical_and(part == 0, u > 0))
        def _():
            send_out(u - 1)

        @pl.when(part == 3)
        def _():
            pack(u)
            hand_out(u)
            send_filter(u)

    last = UNITS - 1
    send_out(last)
    first_ref[...] = g_out[0, :, 0:B]
    for u in range(UNITS):
        gathered(1, u, r_ref)
        rows = pl.ds(UNIT * u, UNIT)
        pltpu.make_async_copy(g_out.at[dp, rows], h_ref.at[dp, rows], g_own.at[u]).wait()
        some = h_ref.at[0:7, rows]
        for sem in (g_send, g_recv):
            wait_for(some, sem.at[u])
        wait_for(staged.at[u], hand_send.at[0, u])
        wait_for(staged.at[u], hand_send.at[1, u])
        wait_for(come.at[u, 0 : CHIPS - 1], send.at[0, u])
        wait_for(come.at[u, 0 : CHIPS - 1], send.at[1, u])


def exchange(sent, filter_taps, skip_gain):
    sent = sent.reshape(UNITS, 2, CHIPS, BLOCK, B)
    lags = filter_taps.shape[0]
    share = UNITS * UNIT
    vmem = pl.BlockSpec(memory_space=pltpu.VMEM)
    anywhere = pl.BlockSpec(memory_space=pl.ANY)
    return pl.pallas_call(
        exchange_kernel,
        in_specs=[anywhere, anywhere, pl.BlockSpec(memory_space=pltpu.SMEM)],
        out_specs=[anywhere, anywhere, vmem],
        out_shape=[
            jax.ShapeDtypeStruct((UNITS, CHIPS, 2, BLOCK, B), BF16),
            jax.ShapeDtypeStruct((8, share, lags // 8), F32),
            jax.ShapeDtypeStruct((share, B), F32),
        ],
        scratch_shapes=[
            pltpu.VMEM(filter_taps.shape, F32),
            pltpu.VMEM((UNITS, CHIPS, 2, BLOCK, B), BF16),
            pltpu.VMEM((UNITS, CHIPS, 2, BLOCK, B), BF16),
            pltpu.VMEM((UNITS, CHIPS, BLOCK, B), BF16),
            pltpu.VMEM((UNITS, CHIPS, 2, BLOCK, B), BF16),
            pltpu.VMEM((8, share, lags // 8), F32),
            pltpu.VMEM((share, 1, lags), F32),
            pltpu.VMEM((UNIT, B + 8, B), F32),
            pltpu.VMEM((UNIT, B + 8, B), F32),
            pltpu.VMEM((UNIT, B, B), F32),
            pltpu.VMEM((UNIT, B, B), F32),
            pltpu.VMEM((UNIT, 1, lags), F32),
            pltpu.VMEM((2, 2 * B, 2 * B), BF16),
            pltpu.VMEM((2, 2 * B, 2 * B), BF16),
            pltpu.VMEM((2, lags, B), BF16),
            pltpu.VMEM((2, B, lags), BF16),
            pltpu.VMEM((256, 256), BF16),
            pltpu.VMEM((B, B), BF16),
            pltpu.SemaphoreType.DMA((UNITS,)),
            pltpu.SemaphoreType.DMA((2, UNITS)),
            pltpu.SemaphoreType.DMA((2, UNITS)),
            pltpu.SemaphoreType.DMA((2, UNITS)),
            pltpu.SemaphoreType.DMA((2, UNITS)),
            pltpu.SemaphoreType.DMA((2, UNITS)),
            pltpu.SemaphoreType.DMA((UNITS,)),
            pltpu.SemaphoreType.DMA((UNITS,)),
            pltpu.SemaphoreType.DMA((UNITS,)),
            pltpu.SemaphoreType.DMA,
        ],
        compiler_params=pltpu.CompilerParams(
            collective_id=0, has_side_effects=True, vmem_limit_bytes=LIMIT
        ),
        name="exchange",
    )(sent, filter_taps, skip_gain)


def finish_kernel(r_ref, k_ref, v_ref, o_ref, dq_ref, dk_ref, dv_ref):
    rows, cols = iotas((B, B))
    eye = one_hot(rows == cols)
    for m in range(k_ref.shape[1] // 256):
        for half in range(2):
            at = slice(256 * m + 128 * half, 256 * m + 128 * half + 128)
            mixed = r_ref[:, half, :, m // 2, m % 2].astype(F32)
            sorted_rows = jnp.concatenate(
                [
                    mixed[u, dp, which * UNIT : which * UNIT + UNIT]
                    for which in range(2)
                    for dp in range(4)
                    for u in range(UNITS)
                ],
                axis=0,
            ).astype(BF16)
            both = dot_nt(eye, sorted_rows)
            conv, back = both[:, :B], both[:, B:]
            dq_ref[:, at] = (o_ref[:, at].astype(F32) * conv).astype(BF16)
            dk_ref[:, at] = (v_ref[:, at].astype(F32) * back).astype(BF16)
            dv_ref[:, at] = (k_ref[:, at].astype(F32) * back).astype(BF16)


def finish(received, k, v, o):
    width = k.shape[1]
    step = 2048
    spec = pl.BlockSpec((B, step), lambda i: (0, i))
    return pl.pallas_call(
        finish_kernel,
        grid=(width // step,),
        in_specs=[
            pl.BlockSpec(
                (UNITS, 2, 4, step // 512, 2, BLOCK, B),
                lambda i: (0, i * step // 2048, 0, i % (2048 // step), 0, 0, 0),
            )
        ]
        + [spec] * 3,
        out_specs=[spec] * 3,
        out_shape=[jax.ShapeDtypeStruct((B, width), BF16)] * 3,
        name="finish",
    )(received, k, v, o)


def per_device(query_rows, key_rows, value_rows, grad_out, filter_taps, skip_gain):
    q, k, v, o = query_rows[0], key_rows[0], value_rows[0], grad_out[0]
    sent = prepare(q, k, v, o)
    returned, filter_rows, first_lags = exchange(sent, filter_taps, skip_gain)
    returned = returned.reshape(UNITS, 4, 4, 4, 2, BLOCK, B)
    dq, dk, dv = finish(returned, k, v, o)
    filter_part = jnp.transpose(filter_rows.reshape(-1, filter_rows.shape[2]))
    return dq[None], dk[None], dv[None], filter_part, first_lags[:, 0]


def solution(mesh):
    rows = P("dp", "ctx", None)
    return jax.shard_map(
        per_device,
        mesh=mesh,
        in_specs=(rows, rows, rows, rows, P(None, "ctx"), P("ctx")),
        out_specs=(rows, rows, rows, P("dp", "ctx"), P(("ctx", "dp"))),
        check_vma=False,
    )
```

```python
import functools

import jax
import jax.numpy as jnp
from jax import lax
from jax.experimental import pallas as pl
from jax.experimental.pallas import tpu as pltpu
from jax.sharding import PartitionSpec as P

F32 = jnp.float32
BF16 = jnp.bfloat16
B = 128
LIMIT = 56 * 1024 * 1024


def dot_nn(a, b):
    return lax.dot_general(a, b, (((1,), (0,)), ((), ())), preferred_element_type=F32)


def dot_nt(a, b):
    return lax.dot_general(a, b, (((1,), (1,)), ((), ())), preferred_element_type=F32)


def iotas(shape):
    return (
        lax.broadcasted_iota(jnp.int32, shape, 0),
        lax.broadcasted_iota(jnp.int32, shape, 1),
    )


def one_hot(cond):
    return jnp.where(cond, 1.0, 0.0).astype(BF16)


def product(a, b):
    return (a.astype(F32) * b.astype(F32)).astype(BF16)


UNITS = 4
UNIT = 8
BLOCK = 2 * UNIT
PADDED = B + 16
CHIPS = 64
MESH = pl.DeviceIdType.MESH


def prepare_kernel(q_ref, k_ref, v_ref, o_ref, s_ref):
    rows, cols = iotas((256, 256))
    place = one_hot(
        cols == (rows // 8 % 2) * 128 + (rows // 64) * 32 + (rows // 16 % 4) * 8 + rows % 8
    )
    for m in range(q_ref.shape[1] // 256):
        for half in range(2):
            at = slice(256 * m + 128 * half, 256 * m + 128 * half + 128)
            both = jnp.concatenate(
                [product(k_ref[:, at], v_ref[:, at]), product(o_ref[:, at], q_ref[:, at])], axis=1
            )
            turned = dot_nt(place, both).astype(BF16).reshape(4, UNITS, BLOCK, B)
            for u in range(UNITS):
                s_ref[u, m % 2, half, :, m // 2] = turned[:, u]


def prepare(q, k, v, o):
    step = 2048
    spec = pl.BlockSpec((B, step), lambda i: (0, i))
    return pl.pallas_call(
        prepare_kernel,
        grid=(q.shape[1] // step,),
        in_specs=[spec] * 4,
        out_specs=pl.BlockSpec(
            (UNITS, 2, 2, 4, step // 512, BLOCK, B),
            lambda i: (0, 0, i * step // 2048, 0, i % (2048 // step), 0, 0),
        ),
        out_shape=jax.ShapeDtypeStruct((UNITS, 2, 4, 4, 4, BLOCK, B), BF16),
        name="prepare",
    )(q, k, v, o)


def exchange_kernel(
    s_ref, f_any, skip_ref, r_ref, h_ref, first_ref,
    f_ref, going, come, staged, leaving,
    g_out, taps, xs, gs, ys, zs, gu, x2s, g2s, g2ms, t_rows_s, t_cols_s, flip,
    own_sems, hand_send, hand_recv, send, recv, stay, g_send, g_recv, g_own, f_sem,
):
    lags = f_ref.shape[0]
    blocks = lags // B
    ctx, dp = lax.axis_index("ctx"), lax.axis_index("dp")
    core = ctx % 2
    x, y, z = (ctx // 8) * 2 + dp // 4, dp % 4, (ctx // 2) % 4
    chip = x * 16 + y * 4 + z
    mate = {"ctx": ctx + 1 - 2 * core, "dp": dp}

    def peer(n):
        m = lax.rem(n * 27, CHIPS)
        x_there = lax.rem(x + lax.div(m, 16), 4)
        y_there = lax.rem(y + lax.div(m, 4), 4)
        z_there = lax.rem(z + m, 4)
        x_high = lax.div(x_there, 2)
        device = {
            "ctx": x_high * 8 + z_there * 2 + core,
            "dp": (x_there - 2 * x_high) * 4 + y_there,
        }
        return device, x_there * 16 + y_there * 4 + z_there

    def remote(source, target, sems, device):
        pltpu.make_async_remote_copy(
            src_ref=source,
            dst_ref=target,
            send_sem=sems[0],
            recv_sem=sems[1],
            device_id=device,
            device_id_type=MESH,
        ).start()

    def wait_for(some, sem):
        pltpu.make_async_copy(some, some, sem).wait()

    barrier = pltpu.get_barrier_semaphore()
    pl.semaphore_signal(barrier, 1, device_id=mate, device_id_type=MESH)

    @pl.loop(1, CHIPS)
    def _(n):
        pl.semaphore_signal(barrier, 1, device_id=peer(n)[0], device_id_type=MESH)

    def own_copy(u):
        return pltpu.make_async_copy(s_ref.at[u, core], going.at[u, :, core], own_sems.at[u])

    filter_copy = pltpu.make_async_copy(f_any, f_ref, f_sem)
    for u in range(UNITS):
        own_copy(u).start()
    filter_copy.start()
    pl.semaphore_wait(barrier, CHIPS)
    for u in range(UNITS):
        remote(s_ref.at[u, 1 - core], going.at[u, :, core], (hand_send.at[0, u], hand_recv.at[0, u]), mate)

    def spread(way, u, source, target):
        @pl.loop(1, CHIPS)
        def _(n):
            device, there = peer(n)
            remote(source.at[u, there], target.at[u, chip], (send.at[way, u], recv.at[way, u]), device)

        pltpu.make_async_copy(source.at[u, chip], target.at[u, chip], stay.at[way, u]).start()

    def gathered(way, u, target):
        wait_for(target.at[u, chip], stay.at[way, u])
        wait_for(target.at[u, 0 : CHIPS - 1], recv.at[way, u])

    @pl.loop(0, UNITS)
    def _(u):
        own_copy(u).wait()
        wait_for(going.at[u, :, 1 - core], hand_recv.at[0, u])
        spread(0, u, going, come)

    share = UNITS * UNIT
    first = dp * share
    filter_copy.wait()
    rows, cols = iotas((share, f_ref.shape[1]))
    pick = one_hot(cols == rows + first)
    for m in range(lags // 256):
        at = slice(256 * m, 256 * m + 256)
        taps[:, :, at] = dot_nt(pick, f_ref[at, :].astype(BF16)).reshape(share, 1, 256)
    rows, cols = iotas((B, B))
    flip[...] = one_hot(rows + cols == B - 1)
    for d in range(UNIT):
        xs[PADDED * d : PADDED * d + 8, :] = jnp.zeros((8, B), F32)
        gs[PADDED * d + B : PADDED * d + PADDED, :] = jnp.zeros((16, B), F32)
    x2s[:, 0:B, :] = jnp.zeros((2, B, 2 * B), BF16)
    g2s[:, B : 2 * B, :] = jnp.zeros((2, B, 2 * B), BF16)
    g2ms[:, B : 2 * B, :] = jnp.zeros((2, B, 2 * B), BF16)

    def unpack(u):
        @pl.loop(0, 4)
        def _(iz):
            for ic in range(2):
                for i in range(16):
                    block = come[u, 4 * i + iz, ic].astype(F32)
                    row = (i // 8) * 64 + iz * 16 + ic * 8 + i % 8
                    xs[pl.ds(row + 8, UNIT, PADDED), :] = block[:UNIT]
                    gs[pl.ds(row, UNIT, PADDED), :] = block[UNIT:]

    def pack(u):
        @pl.loop(0, 4)
        def _(iz):
            for ic in range(2):
                blocks_out = []
                for i in range(16):
                    row = (i // 8) * 64 + iz * 16 + ic * 8 + i % 8
                    pair = [ref[pl.ds(row, UNIT, B), :] for ref in (ys, zs)]
                    blocks_out.append(jnp.concatenate(pair, axis=0).astype(BF16))

                @pl.when(core == ic)
                def _():
                    for i in range(16):
                        leaving[u, 4 * i + iz, ic] = blocks_out[i]

                @pl.when(core != ic)
                def _():
                    for i in range(16):
                        staged[u, 4 * i + iz] = blocks_out[i]

        at = pl.multiple_of(u * UNIT, UNIT)
        filter_rows = gu[...].reshape(UNIT, lags)
        for i in range(8):
            g_out[i, pl.ds(at, UNIT), :] = filter_rows[:, 256 * i : 256 * i + 256]

    def send_filter(u):
        at = pl.multiple_of(u * UNIT, UNIT)
        rows = pl.ds(at, UNIT)
        pltpu.make_async_copy(g_out.at[dp, rows], h_ref.at[dp, rows], g_own.at[u]).start()

        @pl.loop(1, 8)
        def _(n):
            there = (dp + n) % 8
            remote(
                g_out.at[there, rows],
                h_ref.at[dp, rows],
                (g_send.at[u], g_recv.at[u]),
                {"ctx": ctx, "dp": there},
            )

    def hand_out(u):
        remote(staged.at[u], leaving.at[u, :, core], (hand_send.at[1, u], hand_recv.at[1, u]), mate)

    def send_out(u):
        wait_for(leaving.at[u, :, 1 - core], hand_recv.at[1, u])
        spread(1, u, leaving, r_ref)

    def channel(u, d, way):
        x2, g2, g2m, t_rows, t_cols = (
            ref.at[way] for ref in (x2s, g2s, g2ms, t_rows_s, t_cols_s)
        )
        base = pl.multiple_of(d * PADDED, 8)
        x = xs[pl.ds(base + 8, B), :]
        x2[B : 2 * B, 0:B] = x.astype(BF16)
        x2[B : 2 * B, B : 2 * B] = xs[pl.ds(base, B), :].astype(BF16)
        g = gs[pl.ds(base, B), :]
        g2[0:B, 0:B] = g.astype(BF16)
        g2[0:B, B : 2 * B] = gs[pl.ds(base + 8, B), :].astype(BF16)
        rows, cols = iotas((B, B))
        low = cols >= rows
        before = jnp.zeros((B, B), F32)
        for k in range(blocks):
            line = taps[u * UNIT + d, :, B * k : B * k + B]
            turned = pltpu.roll(jnp.broadcast_to(line, (B, B)), 0, 1, stride=1, stride_axis=0)
            t = jnp.where(low, turned, before).astype(BF16)
            t_rows[B * k : B * k + B, :] = t
            t_cols[:, B * k : B * k + B] = t
            before = turned
        gain = skip_ref[first + u * UNIT + d]
        y = gain * x
        z = gain * g
        for j in range(blocks // 2):
            y = y + dot_nn(x2[B - 16 * j : 2 * B - 16 * j, :], t_rows[256 * j : 256 * j + 256, :])
            z = z + dot_nt(g2[16 * j : 16 * j + B, :], t_cols[:, 256 * j : 256 * j + 256])
        at = pl.multiple_of(d * B, B)
        ys[pl.ds(at, B), :] = y
        zs[pl.ds(at, B), :] = z
        moved = pltpu.roll(gs[pl.ds(base, PADDED), :], B // 2, 1)
        _, lanes = iotas((B + 8, B))
        moved = jnp.where(lanes < B // 2, moved[: B + 8], moved[8:])
        g2m[0:B, 0:B] = moved[:B].astype(BF16)
        g2m[0:B, B : 2 * B] = moved[8:].astype(BF16)
        x_turned = dot_nt(flip[...], x2[B : 2 * B, 0:B]).astype(BF16)
        x_turned = jnp.concatenate([x_turned[B // 2 :], x_turned[: B // 2]], axis=1)
        rows, cols = iotas((B // 2, B))
        keep = cols + rows >= B // 2 - 1
        after = jnp.zeros((B // 2, B), F32)
        for j in reversed(range(blocks // 2)):
            at = slice(16 * j, 16 * j + B)
            pair = dot_nn(x_turned, jnp.concatenate([g2[at, :], g2m[at, :]], axis=0))
            for k, part in ((2 * j + 1, pair[:, B:]), (2 * j, pair[:, :B])):
                mixed = jnp.where(keep, part, after)
                turned = pltpu.roll(mixed, B // 2 + 1, 1, stride=1, stride_axis=0)
                gu[d, :, B * k : B * k + B] = jnp.sum(turned, axis=0, keepdims=True)
                after = part

    @pl.loop(0, 4 * UNITS)
    def _(step):
        u, part = step // 4, step % 4

        @pl.when(part == 0)
        def _():
            gathered(0, u, come)
            unpack(u)

        for d in range(2):
            channel(u, part * 2 + d, d)

        @pl.when(jnp.logical_and(part == 0, u > 0))
        def _():
            send_out(u - 1)

        @pl.when(part == 3)
        def _():
            pack(u)
            hand_out(u)
            send_filter(u)

    last = UNITS - 1
    send_out(last)
    first_ref[...] = g_out[0, :, 0:B]
    for u in range(UNITS):
        gathered(1, u, r_ref)
        rows = pl.ds(UNIT * u, UNIT)
        pltpu.make_async_copy(g_out.at[dp, rows], h_ref.at[dp, rows], g_own.at[u]).wait()
        some = h_ref.at[0:7, rows]
        for sem in (g_send, g_recv):
            wait_for(some, sem.at[u])
        wait_for(staged.at[u], hand_send.at[0, u])
        wait_for(staged.at[u], hand_send.at[1, u])
        wait_for(come.at[u, 0 : CHIPS - 1], send.at[0, u])
        wait_for(come.at[u, 0 : CHIPS - 1], send.at[1, u])


def exchange(sent, filter_taps, skip_gain):
    sent = sent.reshape(UNITS, 2, CHIPS, BLOCK, B)
    lags = filter_taps.shape[0]
    share = UNITS * UNIT
    vmem = pl.BlockSpec(memory_space=pltpu.VMEM)
    anywhere = pl.BlockSpec(memory_space=pl.ANY)
    return pl.pallas_call(
        exchange_kernel,
        in_specs=[anywhere, anywhere, pl.BlockSpec(memory_space=pltpu.SMEM)],
        out_specs=[anywhere, anywhere, vmem],
        out_shape=[
            jax.ShapeDtypeStruct((UNITS, CHIPS, 2, BLOCK, B), BF16),
            jax.ShapeDtypeStruct((8, share, lags // 8), F32),
            jax.ShapeDtypeStruct((share, B), F32),
        ],
        scratch_shapes=[
            pltpu.VMEM(filter_taps.shape, F32),
            pltpu.VMEM((UNITS, CHIPS, 2, BLOCK, B), BF16),
            pltpu.VMEM((UNITS, CHIPS, 2, BLOCK, B), BF16),
            pltpu.VMEM((UNITS, CHIPS, BLOCK, B), BF16),
            pltpu.VMEM((UNITS, CHIPS, 2, BLOCK, B), BF16),
            pltpu.VMEM((8, share, lags // 8), F32),
            pltpu.VMEM((share, 1, lags), F32),
            pltpu.VMEM((UNIT * PADDED, B), F32),
            pltpu.VMEM((UNIT * PADDED, B), F32),
            pltpu.VMEM((UNIT * B, B), F32),
            pltpu.VMEM((UNIT * B, B), F32),
            pltpu.VMEM((UNIT, 1, lags), F32),
            pltpu.VMEM((2, 2 * B, 2 * B), BF16),
            pltpu.VMEM((2, 2 * B, 2 * B), BF16),
            pltpu.VMEM((2, 2 * B, 2 * B), BF16),
            pltpu.VMEM((2, lags, B), BF16),
            pltpu.VMEM((2, B, lags), BF16),
            pltpu.VMEM((B, B), BF16),
            pltpu.SemaphoreType.DMA((UNITS,)),
            pltpu.SemaphoreType.DMA((2, UNITS)),
            pltpu.SemaphoreType.DMA((2, UNITS)),
            pltpu.SemaphoreType.DMA((2, UNITS)),
            pltpu.SemaphoreType.DMA((2, UNITS)),
            pltpu.SemaphoreType.DMA((2, UNITS)),
            pltpu.SemaphoreType.DMA((UNITS,)),
            pltpu.SemaphoreType.DMA((UNITS,)),
            pltpu.SemaphoreType.DMA((UNITS,)),
            pltpu.SemaphoreType.DMA,
        ],
        compiler_params=pltpu.CompilerParams(
            collective_id=0, has_side_effects=True, vmem_limit_bytes=LIMIT
        ),
        name="exchange",
    )(sent, filter_taps, skip_gain)


def finish_kernel(r_ref, k_ref, v_ref, o_ref, h_ref, first_ref, dq_ref, dk_ref, dv_ref, df_ref, ds_ref):
    @pl.when(pl.program_id(0) == 0)
    def _():
        df_ref[...] = jnp.transpose(h_ref[...])
        ds_ref[...] = jnp.transpose(first_ref[...])[0:1]

    rows, cols = iotas((B, B))
    eye = one_hot(rows == cols)
    for m in range(k_ref.shape[1] // 256):
        for half in range(2):
            at = slice(256 * m + 128 * half, 256 * m + 128 * half + 128)
            mixed = r_ref[:, half, :, m // 2, m % 2].astype(F32)
            sorted_rows = jnp.concatenate(
                [
                    mixed[u, dp, which * UNIT : which * UNIT + UNIT]
                    for which in range(2)
                    for dp in range(4)
                    for u in range(UNITS)
                ],
                axis=0,
            ).astype(BF16)
            both = dot_nt(eye, sorted_rows)
            conv, back = both[:, :B], both[:, B:]
            dq_ref[:, at] = (o_ref[:, at].astype(F32) * conv).astype(BF16)
            dk_ref[:, at] = (v_ref[:, at].astype(F32) * back).astype(BF16)
            dv_ref[:, at] = (k_ref[:, at].astype(F32) * back).astype(BF16)


def finish(received, k, v, o, filter_rows, first_lags):
    channels, lags = filter_rows.shape
    width = k.shape[1]
    step = 2048
    spec = pl.BlockSpec((B, step), lambda i: (0, i))
    return pl.pallas_call(
        finish_kernel,
        grid=(width // step,),
        in_specs=[
            pl.BlockSpec(
                (UNITS, 2, 4, step // 512, 2, BLOCK, B),
                lambda i: (0, i * step // 2048, 0, i % (2048 // step), 0, 0, 0),
            )
        ]
        + [spec] * 3
        + [pl.BlockSpec((channels, lags), lambda i: (0, 0)), pl.BlockSpec(first_lags.shape, lambda i: (0, 0))],
        out_specs=[spec] * 3
        + [pl.BlockSpec((lags, channels), lambda i: (0, 0)), pl.BlockSpec((1, first_lags.shape[0]), lambda i: (0, 0))],
        out_shape=[jax.ShapeDtypeStruct((B, width), BF16)] * 3
        + [
            jax.ShapeDtypeStruct((lags, channels), F32),
            jax.ShapeDtypeStruct((1, first_lags.shape[0]), F32),
        ],
        name="finish",
    )(received, k, v, o, filter_rows, first_lags)


def per_device(query_rows, key_rows, value_rows, grad_out, filter_taps, skip_gain):
    q, k, v, o = query_rows[0], key_rows[0], value_rows[0], grad_out[0]
    sent = prepare(q, k, v, o)
    returned, filter_rows, first_lags = exchange(sent, filter_taps, skip_gain)
    returned = returned.reshape(UNITS, 4, 4, 4, 2, BLOCK, B)
    filter_rows = filter_rows.reshape(-1, filter_rows.shape[2])
    dq, dk, dv, d_filter, d_skip = finish(returned, k, v, o, filter_rows, first_lags)
    return dq[None], dk[None], dv[None], d_filter, d_skip[0]


def solution(mesh):
    rows = P("dp", "ctx", None)
    return jax.shard_map(
        per_device,
        mesh=mesh,
        in_specs=(rows, rows, rows, rows, P(None, "ctx"), P("ctx")),
        out_specs=(rows, rows, rows, P("dp", "ctx"), P(("ctx", "dp"))),
        check_vma=False,
    )
```

```python
import functools

import jax
import jax.numpy as jnp
from jax import lax
from jax.experimental import pallas as pl
from jax.experimental.pallas import tpu as pltpu
from jax.sharding import PartitionSpec as P

F32 = jnp.float32
BF16 = jnp.bfloat16
B = 128
LIMIT = 56 * 1024 * 1024


def dot_nn(a, b):
    return lax.dot_general(a, b, (((1,), (0,)), ((), ())), preferred_element_type=F32)


def dot_nt(a, b):
    return lax.dot_general(a, b, (((1,), (1,)), ((), ())), preferred_element_type=F32)


def iotas(shape):
    return (
        lax.broadcasted_iota(jnp.int32, shape, 0),
        lax.broadcasted_iota(jnp.int32, shape, 1),
    )


def one_hot(cond):
    return jnp.where(cond, 1.0, 0.0).astype(BF16)


def product(a, b):
    return (a.astype(F32) * b.astype(F32)).astype(BF16)


UNITS = 4
UNIT = 8
BLOCK = 2 * UNIT
PADDED = B + 16
CHIPS = 64
MESH = pl.DeviceIdType.MESH


def exchange_kernel(
    q_any, k_any, v_any, o_any, f_any, skip_ref, r_ref, h_ref, first_ref,
    q_ref, k_ref, v_ref, o_ref, f_ref, going, prepared, come, staged, leaving,
    g_out, taps, xs, gs, ys, zs, gu, x2s, g2s, g2ms, t_rows_s, t_cols_s, flip, turn,
    load_sems, hand_send, hand_recv, send, recv, stay, g_send, g_recv, g_own, f_sem,
):
    lags = f_ref.shape[0]
    blocks = lags // B
    ctx, dp = lax.axis_index("ctx"), lax.axis_index("dp")
    core = ctx % 2
    x, y, z = (ctx // 8) * 2 + dp // 4, dp % 4, (ctx // 2) % 4
    chip = x * 16 + y * 4 + z
    mate = {"ctx": ctx + 1 - 2 * core, "dp": dp}

    def peer(n):
        m = lax.rem(n * 27, CHIPS)
        x_there = lax.rem(x + lax.div(m, 16), 4)
        y_there = lax.rem(y + lax.div(m, 4), 4)
        z_there = lax.rem(z + m, 4)
        x_high = lax.div(x_there, 2)
        device = {
            "ctx": x_high * 8 + z_there * 2 + core,
            "dp": (x_there - 2 * x_high) * 4 + y_there,
        }
        return device, x_there * 16 + y_there * 4 + z_there

    def remote(source, target, sems, device):
        pltpu.make_async_remote_copy(
            src_ref=source,
            dst_ref=target,
            send_sem=sems[0],
            recv_sem=sems[1],
            device_id=device,
            device_id_type=MESH,
        ).start()

    def wait_for(some, sem):
        pltpu.make_async_copy(some, some, sem).wait()

    half_width = q_ref.shape[1] // 2

    def load(half):
        at = slice(half * half_width, half * half_width + half_width)
        return [
            pltpu.make_async_copy(any_ref.at[:, at], ref.at[:, at], load_sems.at[half, i])
            for i, (any_ref, ref) in enumerate(
                ((k_any, k_ref), (v_any, v_ref), (o_any, o_ref), (q_any, q_ref))
            )
        ]

    for half in range(2):
        for copy in load(half):
            copy.start()

    barrier = pltpu.get_barrier_semaphore()
    pl.semaphore_signal(barrier, 1, device_id=mate, device_id_type=MESH)

    @pl.loop(1, CHIPS)
    def _(n):
        pl.semaphore_signal(barrier, 1, device_id=peer(n)[0], device_id_type=MESH)

    filter_copy = pltpu.make_async_copy(f_any, f_ref, f_sem)
    filter_copy.start()

    rows, cols = iotas((256, 256))
    turn[...] = one_hot(
        cols == (rows // 8 % 2) * 128 + (rows // 64) * 32 + (rows // 16 % 4) * 8 + rows % 8
    )

    def prepare(x_upper):
        @pl.loop(0, 4)
        def _(iz):
            for ic in range(2):
                for x_lower in range(2):
                    start = x_upper * half_width + (iz * 2 + ic) * 256 + x_lower * B
                    at = pl.ds(pl.multiple_of(start, B), B)
                    both = jnp.concatenate(
                        [product(k_ref[:, at], v_ref[:, at]), product(o_ref[:, at], q_ref[:, at])],
                        axis=1,
                    )
                    turned = dot_nt(turn[...], both).astype(BF16).reshape(4, UNITS, BLOCK, B)
                    corner = x_upper * 32 + x_lower * 16 + iz

                    @pl.when(core == ic)
                    def _():
                        for there_y in range(4):
                            for u in range(UNITS):
                                going[u, corner + 4 * there_y, ic] = turned[there_y, u]

                    @pl.when(core != ic)
                    def _():
                        for there_y in range(4):
                            for u in range(UNITS):
                                prepared[u, corner + 4 * there_y] = turned[there_y, u]

    for half in range(2):
        for copy in load(half):
            copy.wait()
        prepare(half)

    pl.semaphore_wait(barrier, CHIPS)
    for u in range(UNITS):
        remote(prepared.at[u], going.at[u, :, core], (hand_send.at[0, u], hand_recv.at[0, u]), mate)

    def spread(way, u, source, target):
        @pl.loop(1, CHIPS)
        def _(n):
            device, there = peer(n)
            remote(source.at[u, there], target.at[u, chip], (send.at[way, u], recv.at[way, u]), device)

        pltpu.make_async_copy(source.at[u, chip], target.at[u, chip], stay.at[way, u]).start()

    def gathered(way, u, target):
        wait_for(target.at[u, chip], stay.at[way, u])
        wait_for(target.at[u, 0 : CHIPS - 1], recv.at[way, u])

    @pl.loop(0, UNITS)
    def _(u):
        wait_for(going.at[u, :, 1 - core], hand_recv.at[0, u])
        spread(0, u, going, come)

    share = UNITS * UNIT
    first = dp * share
    filter_copy.wait()
    rows, cols = iotas((share, f_ref.shape[1]))
    pick = one_hot(cols == rows + first)
    for m in range(lags // 256):
        at = slice(256 * m, 256 * m + 256)
        taps[:, :, at] = dot_nt(pick, f_ref[at, :].astype(BF16)).reshape(share, 1, 256)
    rows, cols = iotas((B, B))
    flip[...] = one_hot(rows + cols == B - 1)
    for d in range(UNIT):
        xs[PADDED * d : PADDED * d + 8, :] = jnp.zeros((8, B), F32)
        gs[PADDED * d + B : PADDED * d + PADDED, :] = jnp.zeros((16, B), F32)
    x2s[:, 0:B, :] = jnp.zeros((2, B, 2 * B), BF16)
    g2s[:, B : 2 * B, :] = jnp.zeros((2, B, 2 * B), BF16)
    g2ms[:, B : 2 * B, :] = jnp.zeros((2, B, 2 * B), BF16)

    def unpack(u):
        @pl.loop(0, 4)
        def _(iz):
            for ic in range(2):
                for i in range(16):
                    block = come[u, 4 * i + iz, ic].astype(F32)
                    row = (i // 8) * 64 + iz * 16 + ic * 8 + i % 8
                    xs[pl.ds(row + 8, UNIT, PADDED), :] = block[:UNIT]
                    gs[pl.ds(row, UNIT, PADDED), :] = block[UNIT:]

    def pack(u):
        @pl.loop(0, 4)
        def _(iz):
            for ic in range(2):
                blocks_out = []
                for i in range(16):
                    row = (i // 8) * 64 + iz * 16 + ic * 8 + i % 8
                    pair = [ref[pl.ds(row, UNIT, B), :] for ref in (ys, zs)]
                    blocks_out.append(jnp.concatenate(pair, axis=0).astype(BF16))

                @pl.when(core == ic)
                def _():
                    for i in range(16):
                        leaving[u, 4 * i + iz, ic] = blocks_out[i]

                @pl.when(core != ic)
                def _():
                    for i in range(16):
                        staged[u, 4 * i + iz] = blocks_out[i]

        at = pl.multiple_of(u * UNIT, UNIT)
        filter_rows = gu[...].reshape(UNIT, lags)
        for i in range(8):
            g_out[i, pl.ds(at, UNIT), :] = filter_rows[:, 256 * i : 256 * i + 256]

    def send_filter(u):
        at = pl.multiple_of(u * UNIT, UNIT)
        rows = pl.ds(at, UNIT)
        pltpu.make_async_copy(g_out.at[dp, rows], h_ref.at[dp, rows], g_own.at[u]).start()

        @pl.loop(1, 8)
        def _(n):
            there = (dp + n) % 8
            remote(
                g_out.at[there, rows],
                h_ref.at[dp, rows],
                (g_send.at[u], g_recv.at[u]),
                {"ctx": ctx, "dp": there},
            )

    def hand_out(u):
        remote(staged.at[u], leaving.at[u, :, core], (hand_send.at[1, u], hand_recv.at[1, u]), mate)

    def send_out(u):
        wait_for(leaving.at[u, :, 1 - core], hand_recv.at[1, u])
        spread(1, u, leaving, r_ref)

    def channel(u, d, way):
        x2, g2, g2m, t_rows, t_cols = (
            ref.at[way] for ref in (x2s, g2s, g2ms, t_rows_s, t_cols_s)
        )
        base = pl.multiple_of(d * PADDED, 8)
        x = xs[pl.ds(base + 8, B), :]
        x2[B : 2 * B, 0:B] = x.astype(BF16)
        x2[B : 2 * B, B : 2 * B] = xs[pl.ds(base, B), :].astype(BF16)
        g = gs[pl.ds(base, B), :]
        g2[0:B, 0:B] = g.astype(BF16)
        g2[0:B, B : 2 * B] = gs[pl.ds(base + 8, B), :].astype(BF16)
        rows, cols = iotas((B, B))
        low = cols >= rows
        before = jnp.zeros((B, B), F32)
        for k in range(blocks):
            line = taps[u * UNIT + d, :, B * k : B * k + B]
            turned = pltpu.roll(jnp.broadcast_to(line, (B, B)), 0, 1, stride=1, stride_axis=0)
            t = jnp.where(low, turned, before).astype(BF16)
            t_rows[B * k : B * k + B, :] = t
            t_cols[:, B * k : B * k + B] = t
            before = turned
        gain = skip_ref[first + u * UNIT + d]
        y = gain * x
        z = gain * g
        for j in range(blocks // 2):
            y = y + dot_nn(x2[B - 16 * j : 2 * B - 16 * j, :], t_rows[256 * j : 256 * j + 256, :])
            z = z + dot_nt(g2[16 * j : 16 * j + B, :], t_cols[:, 256 * j : 256 * j + 256])
        at = pl.multiple_of(d * B, B)
        ys[pl.ds(at, B), :] = y
        zs[pl.ds(at, B), :] = z
        moved = pltpu.roll(gs[pl.ds(base, PADDED), :], B // 2, 1)
        _, lanes = iotas((B + 8, B))
        moved = jnp.where(lanes < B // 2, moved[: B + 8], moved[8:])
        g2m[0:B, 0:B] = moved[:B].astype(BF16)
        g2m[0:B, B : 2 * B] = moved[8:].astype(BF16)
        x_turned = dot_nt(flip[...], x2[B : 2 * B, 0:B]).astype(BF16)
        x_turned = jnp.concatenate([x_turned[B // 2 :], x_turned[: B // 2]], axis=1)
        rows, cols = iotas((B // 2, B))
        keep = cols + rows >= B // 2 - 1
        after = jnp.zeros((B // 2, B), F32)
        for j in reversed(range(blocks // 2)):
            at = slice(16 * j, 16 * j + B)
            pair = dot_nn(x_turned, jnp.concatenate([g2[at, :], g2m[at, :]], axis=0))
            for k, part in ((2 * j + 1, pair[:, B:]), (2 * j, pair[:, :B])):
                mixed = jnp.where(keep, part, after)
                turned = pltpu.roll(mixed, B // 2 + 1, 1, stride=1, stride_axis=0)
                gu[d, :, B * k : B * k + B] = jnp.sum(turned, axis=0, keepdims=True)
                after = part

    @pl.loop(0, 4 * UNITS)
    def _(step):
        u, part = step // 4, step % 4

        @pl.when(part == 0)
        def _():
            gathered(0, u, come)
            unpack(u)

        for d in range(2):
            channel(u, part * 2 + d, d)

        @pl.when(jnp.logical_and(part == 0, u > 0))
        def _():
            send_out(u - 1)

        @pl.when(part == 3)
        def _():
            pack(u)
            hand_out(u)
            send_filter(u)

    last = UNITS - 1
    send_out(last)
    first_ref[...] = g_out[0, :, 0:B]
    for u in range(UNITS):
        gathered(1, u, r_ref)
        rows = pl.ds(UNIT * u, UNIT)
        pltpu.make_async_copy(g_out.at[dp, rows], h_ref.at[dp, rows], g_own.at[u]).wait()
        some = h_ref.at[0:7, rows]
        for sem in (g_send, g_recv):
            wait_for(some, sem.at[u])
        wait_for(staged.at[u], hand_send.at[0, u])
        wait_for(staged.at[u], hand_send.at[1, u])
        wait_for(come.at[u, 0 : CHIPS - 1], send.at[0, u])
        wait_for(come.at[u, 0 : CHIPS - 1], send.at[1, u])


def exchange(q, k, v, o, filter_taps, skip_gain):
    lags = filter_taps.shape[0]
    share = UNITS * UNIT
    vmem = pl.BlockSpec(memory_space=pltpu.VMEM)
    anywhere = pl.BlockSpec(memory_space=pl.ANY)
    return pl.pallas_call(
        exchange_kernel,
        in_specs=[anywhere] * 5 + [pl.BlockSpec(memory_space=pltpu.SMEM)],
        out_specs=[anywhere, anywhere, vmem],
        out_shape=[
            jax.ShapeDtypeStruct((UNITS, CHIPS, 2, BLOCK, B), BF16),
            jax.ShapeDtypeStruct((8, share, lags // 8), F32),
            jax.ShapeDtypeStruct((share, B), F32),
        ],
        scratch_shapes=[
            *[pltpu.VMEM(q.shape, BF16)] * 4,
            pltpu.VMEM(filter_taps.shape, F32),
            pltpu.VMEM((UNITS, CHIPS, 2, BLOCK, B), BF16),
            pltpu.VMEM((UNITS, CHIPS, BLOCK, B), BF16),
            pltpu.VMEM((UNITS, CHIPS, 2, BLOCK, B), BF16),
            pltpu.VMEM((UNITS, CHIPS, BLOCK, B), BF16),
            pltpu.VMEM((UNITS, CHIPS, 2, BLOCK, B), BF16),
            pltpu.VMEM((8, share, lags // 8), F32),
            pltpu.VMEM((share, 1, lags), F32),
            pltpu.VMEM((UNIT * PADDED, B), F32),
            pltpu.VMEM((UNIT * PADDED, B), F32),
            pltpu.VMEM((UNIT * B, B), F32),
            pltpu.VMEM((UNIT * B, B), F32),
            pltpu.VMEM((UNIT, 1, lags), F32),
            pltpu.VMEM((2, 2 * B, 2 * B), BF16),
            pltpu.VMEM((2, 2 * B, 2 * B), BF16),
            pltpu.VMEM((2, 2 * B, 2 * B), BF16),
            pltpu.VMEM((2, lags, B), BF16),
            pltpu.VMEM((2, B, lags), BF16),
            pltpu.VMEM((B, B), BF16),
            pltpu.VMEM((256, 256), BF16),
            pltpu.SemaphoreType.DMA((2, 4)),
            pltpu.SemaphoreType.DMA((2, UNITS)),
            pltpu.SemaphoreType.DMA((2, UNITS)),
            pltpu.SemaphoreType.DMA((2, UNITS)),
            pltpu.SemaphoreType.DMA((2, UNITS)),
            pltpu.SemaphoreType.DMA((2, UNITS)),
            pltpu.SemaphoreType.DMA((UNITS,)),
            pltpu.SemaphoreType.DMA((UNITS,)),
            pltpu.SemaphoreType.DMA((UNITS,)),
            pltpu.SemaphoreType.DMA,
        ],
        compiler_params=pltpu.CompilerParams(
            collective_id=0, has_side_effects=True, vmem_limit_bytes=LIMIT
        ),
        name="exchange",
    )(q, k, v, o, filter_taps, skip_gain)


def finish_kernel(r_ref, k_ref, v_ref, o_ref, h_ref, first_ref, dq_ref, dk_ref, dv_ref, df_ref, ds_ref):
    @pl.when(pl.program_id(0) == 0)
    def _():
        df_ref[...] = jnp.transpose(h_ref[...])
        ds_ref[...] = jnp.transpose(first_ref[...])[0:1]

    rows, cols = iotas((B, B))
    eye = one_hot(rows == cols)
    for m in range(k_ref.shape[1] // 256):
        for half in range(2):
            at = slice(256 * m + 128 * half, 256 * m + 128 * half + 128)
            mixed = r_ref[:, half, :, m // 2, m % 2].astype(F32)
            sorted_rows = jnp.concatenate(
                [
                    mixed[u, dp, which * UNIT : which * UNIT + UNIT]
                    for which in range(2)
                    for dp in range(4)
                    for u in range(UNITS)
                ],
                axis=0,
            ).astype(BF16)
            both = dot_nt(eye, sorted_rows)
            conv, back = both[:, :B], both[:, B:]
            dq_ref[:, at] = (o_ref[:, at].astype(F32) * conv).astype(BF16)
            dk_ref[:, at] = (v_ref[:, at].astype(F32) * back).astype(BF16)
            dv_ref[:, at] = (k_ref[:, at].astype(F32) * back).astype(BF16)


def finish(received, k, v, o, filter_rows, first_lags):
    channels, lags = filter_rows.shape
    width = k.shape[1]
    step = 2048
    spec = pl.BlockSpec((B, step), lambda i: (0, i))
    return pl.pallas_call(
        finish_kernel,
        grid=(width // step,),
        in_specs=[
            pl.BlockSpec(
                (UNITS, 2, 4, step // 512, 2, BLOCK, B),
                lambda i: (0, i * step // 2048, 0, i % (2048 // step), 0, 0, 0),
            )
        ]
        + [spec] * 3
        + [pl.BlockSpec((channels, lags), lambda i: (0, 0)), pl.BlockSpec(first_lags.shape, lambda i: (0, 0))],
        out_specs=[spec] * 3
        + [pl.BlockSpec((lags, channels), lambda i: (0, 0)), pl.BlockSpec((1, first_lags.shape[0]), lambda i: (0, 0))],
        out_shape=[jax.ShapeDtypeStruct((B, width), BF16)] * 3
        + [
            jax.ShapeDtypeStruct((lags, channels), F32),
            jax.ShapeDtypeStruct((1, first_lags.shape[0]), F32),
        ],
        name="finish",
    )(received, k, v, o, filter_rows, first_lags)


def per_device(query_rows, key_rows, value_rows, grad_out, filter_taps, skip_gain):
    q, k, v, o = query_rows[0], key_rows[0], value_rows[0], grad_out[0]
    returned, filter_rows, first_lags = exchange(q, k, v, o, filter_taps, skip_gain)
    returned = returned.reshape(UNITS, 4, 4, 4, 2, BLOCK, B)
    filter_rows = filter_rows.reshape(-1, filter_rows.shape[2])
    dq, dk, dv, d_filter, d_skip = finish(returned, k, v, o, filter_rows, first_lags)
    return dq[None], dk[None], dv[None], d_filter, d_skip[0]


def solution(mesh):
    rows = P("dp", "ctx", None)
    return jax.shard_map(
        per_device,
        mesh=mesh,
        in_specs=(rows, rows, rows, rows, P(None, "ctx"), P("ctx")),
        out_specs=(rows, rows, rows, P("dp", "ctx"), P(("ctx", "dp"))),
        check_vma=False,
    )
```

```python
import functools

import jax
import jax.numpy as jnp
from jax import lax
from jax.experimental import pallas as pl
from jax.experimental.pallas import tpu as pltpu
from jax.sharding import PartitionSpec as P

F32 = jnp.float32
BF16 = jnp.bfloat16
B = 128
LIMIT = 56 * 1024 * 1024


def dot_nn(a, b):
    return lax.dot_general(a, b, (((1,), (0,)), ((), ())), preferred_element_type=F32)


def dot_nt(a, b):
    return lax.dot_general(a, b, (((1,), (1,)), ((), ())), preferred_element_type=F32)


def iotas(shape):
    return (
        lax.broadcasted_iota(jnp.int32, shape, 0),
        lax.broadcasted_iota(jnp.int32, shape, 1),
    )


def one_hot(cond):
    return jnp.where(cond, 1.0, 0.0).astype(BF16)


def product(a, b):
    return (a.astype(F32) * b.astype(F32)).astype(BF16)


UNITS = 4
UNIT = 8
BLOCK = 2 * UNIT
PADDED = B + 16
CHIPS = 64
MESH = pl.DeviceIdType.MESH


def exchange_kernel(
    q_any, k_any, v_any, o_any, f_any, skip_ref, r_ref, h_ref, first_ref,
    q_ref, k_ref, v_ref, o_ref, f_ref, going, come, leaving,
    g_out, taps, xs, gs, ys, zs, gu, x2s, g2s, g2ms, t_rows_s, t_cols_s, flip, turn,
    load_sems, hand_send, hand_recv, send, recv, stay, g_send, g_recv, g_own, f_sem,
):
    lags = f_ref.shape[0]
    blocks = lags // B
    ctx, dp = lax.axis_index("ctx"), lax.axis_index("dp")
    core = ctx % 2
    x, y, z = (ctx // 8) * 2 + dp // 4, dp % 4, (ctx // 2) % 4
    chip = x * 16 + y * 4 + z
    mate = {"ctx": ctx + 1 - 2 * core, "dp": dp}

    def slot(ic):
        return ic + lax.rem(core + ic, 2) * (2 - ic)

    def peer(n):
        m = lax.rem(n * 27, CHIPS)
        x_there = lax.rem(x + lax.div(m, 16), 4)
        y_there = lax.rem(y + lax.div(m, 4), 4)
        z_there = lax.rem(z + m, 4)
        x_high = lax.div(x_there, 2)
        device = {
            "ctx": x_high * 8 + z_there * 2 + core,
            "dp": (x_there - 2 * x_high) * 4 + y_there,
        }
        return device, x_there * 16 + y_there * 4 + z_there

    def remote(source, target, sems, device):
        pltpu.make_async_remote_copy(
            src_ref=source,
            dst_ref=target,
            send_sem=sems[0],
            recv_sem=sems[1],
            device_id=device,
            device_id_type=MESH,
        ).start()

    def wait_for(some, sem):
        pltpu.make_async_copy(some, some, sem).wait()

    half_width = q_ref.shape[1] // 2

    def load(half):
        at = slice(half * half_width, half * half_width + half_width)
        return [
            pltpu.make_async_copy(any_ref.at[:, at], ref.at[:, at], load_sems.at[half, i])
            for i, (any_ref, ref) in enumerate(
                ((k_any, k_ref), (v_any, v_ref), (o_any, o_ref), (q_any, q_ref))
            )
        ]

    for half in range(2):
        for copy in load(half):
            copy.start()

    barrier = pltpu.get_barrier_semaphore()
    pl.semaphore_signal(barrier, 1, device_id=mate, device_id_type=MESH)

    @pl.loop(1, CHIPS)
    def _(n):
        pl.semaphore_signal(barrier, 1, device_id=peer(n)[0], device_id_type=MESH)

    filter_copy = pltpu.make_async_copy(f_any, f_ref, f_sem)
    filter_copy.start()

    rows, cols = iotas((256, 256))
    turn[...] = one_hot(
        cols == (rows // 8 % 2) * 128 + (rows // 64) * 32 + (rows // 16 % 4) * 8 + rows % 8
    )

    def prepare(x_upper):
        @pl.loop(0, 4)
        def _(iz):
            for ic in range(2):
                for x_lower in range(2):
                    start = x_upper * half_width + (iz * 2 + ic) * 256 + x_lower * B
                    at = pl.ds(pl.multiple_of(start, B), B)
                    both = jnp.concatenate(
                        [product(k_ref[:, at], v_ref[:, at]), product(o_ref[:, at], q_ref[:, at])],
                        axis=1,
                    )
                    turned = dot_nt(turn[...], both).astype(BF16).reshape(4, UNITS, BLOCK, B)
                    corner = x_upper * 32 + x_lower * 16 + iz

                    for there_y in range(4):
                        for u in range(UNITS):
                            going[u, corner + 4 * there_y, slot(ic)] = turned[there_y, u]

    for half in range(2):
        for copy in load(half):
            copy.wait()
        prepare(half)

    pl.semaphore_wait(barrier, CHIPS)
    for u in range(UNITS):
        remote(going.at[u, :, 2], going.at[u, :, core], (hand_send.at[0, u], hand_recv.at[0, u]), mate)

    def spread(way, u, source, target):
        @pl.loop(1, CHIPS)
        def _(n):
            device, there = peer(n)
            remote(source.at[u, there, 0:2], target.at[u, chip], (send.at[way, u], recv.at[way, u]), device)

        pltpu.make_async_copy(source.at[u, chip, 0:2], target.at[u, chip], stay.at[way, u]).start()

    def gathered(way, u, target):
        wait_for(target.at[u, chip], stay.at[way, u])
        wait_for(target.at[u, 0 : CHIPS - 1], recv.at[way, u])

    @pl.loop(0, UNITS)
    def _(u):
        wait_for(going.at[u, :, 1 - core], hand_recv.at[0, u])
        spread(0, u, going, come)

    share = UNITS * UNIT
    first = dp * share
    filter_copy.wait()
    rows, cols = iotas((share, f_ref.shape[1]))
    pick = one_hot(cols == rows + first)
    for m in range(lags // 256):
        at = slice(256 * m, 256 * m + 256)
        taps[:, :, at] = dot_nt(pick, f_ref[at, :].astype(BF16)).reshape(share, 1, 256)
    rows, cols = iotas((B, B))
    flip[...] = one_hot(rows + cols == B - 1)
    for d in range(UNIT):
        xs[PADDED * d : PADDED * d + 8, :] = jnp.zeros((8, B), F32)
        gs[PADDED * d + B : PADDED * d + PADDED, :] = jnp.zeros((16, B), F32)
    x2s[:, 0:B, :] = jnp.zeros((2, B, 2 * B), BF16)
    g2s[:, B : 2 * B, :] = jnp.zeros((2, B, 2 * B), BF16)
    g2ms[:, B : 2 * B, :] = jnp.zeros((2, B, 2 * B), BF16)

    def unpack(u):
        @pl.loop(0, 4)
        def _(iz):
            for ic in range(2):
                for i in range(16):
                    block = come[u, 4 * i + iz, ic].astype(F32)
                    row = (i // 8) * 64 + iz * 16 + ic * 8 + i % 8
                    xs[pl.ds(row + 8, UNIT, PADDED), :] = block[:UNIT]
                    gs[pl.ds(row, UNIT, PADDED), :] = block[UNIT:]

    def pack(u):
        @pl.loop(0, 4)
        def _(iz):
            for ic in range(2):
                blocks_out = []
                for i in range(16):
                    row = (i // 8) * 64 + iz * 16 + ic * 8 + i % 8
                    pair = [ref[pl.ds(row, UNIT, B), :] for ref in (ys, zs)]
                    blocks_out.append(jnp.concatenate(pair, axis=0).astype(BF16))

                for i in range(16):
                    leaving[u, 4 * i + iz, slot(ic)] = blocks_out[i]

        at = pl.multiple_of(u * UNIT, UNIT)
        filter_rows = gu[...].reshape(UNIT, lags)
        for i in range(8):
            g_out[i, pl.ds(at, UNIT), :] = filter_rows[:, 256 * i : 256 * i + 256]

    def send_filter(u):
        at = pl.multiple_of(u * UNIT, UNIT)
        rows = pl.ds(at, UNIT)
        pltpu.make_async_copy(g_out.at[dp, rows], h_ref.at[dp, rows], g_own.at[u]).start()

        @pl.loop(1, 8)
        def _(n):
            there = (dp + n) % 8
            remote(
                g_out.at[there, rows],
                h_ref.at[dp, rows],
                (g_send.at[u], g_recv.at[u]),
                {"ctx": ctx, "dp": there},
            )

    def hand_out(u):
        remote(leaving.at[u, :, 2], leaving.at[u, :, core], (hand_send.at[1, u], hand_recv.at[1, u]), mate)

    def send_out(u):
        wait_for(leaving.at[u, :, 1 - core], hand_recv.at[1, u])
        spread(1, u, leaving, r_ref)

    def channel(u, d, way):
        x2, g2, g2m, t_rows, t_cols = (
            ref.at[way] for ref in (x2s, g2s, g2ms, t_rows_s, t_cols_s)
        )
        base = pl.multiple_of(d * PADDED, 8)
        x = xs[pl.ds(base + 8, B), :]
        x2[B : 2 * B, 0:B] = x.astype(BF16)
        x2[B : 2 * B, B : 2 * B] = xs[pl.ds(base, B), :].astype(BF16)
        g = gs[pl.ds(base, B), :]
        g2[0:B, 0:B] = g.astype(BF16)
        g2[0:B, B : 2 * B] = gs[pl.ds(base + 8, B), :].astype(BF16)
        rows, cols = iotas((B, B))
        low = cols >= rows
        before = jnp.zeros((B, B), F32)
        for k in range(blocks):
            line = taps[u * UNIT + d, :, B * k : B * k + B]
            turned = pltpu.roll(jnp.broadcast_to(line, (B, B)), 0, 1, stride=1, stride_axis=0)
            t = jnp.where(low, turned, before).astype(BF16)
            t_rows[B * k : B * k + B, :] = t
            t_cols[:, B * k : B * k + B] = t
            before = turned
        gain = skip_ref[first + u * UNIT + d]
        y = gain * x
        z = gain * g
        for j in range(blocks // 2):
            y = y + dot_nn(x2[B - 16 * j : 2 * B - 16 * j, :], t_rows[256 * j : 256 * j + 256, :])
            z = z + dot_nt(g2[16 * j : 16 * j + B, :], t_cols[:, 256 * j : 256 * j + 256])
        at = pl.multiple_of(d * B, B)
        ys[pl.ds(at, B), :] = y
        zs[pl.ds(at, B), :] = z
        moved = pltpu.roll(gs[pl.ds(base, PADDED), :], B // 2, 1)
        _, lanes = iotas((B + 8, B))
        moved = jnp.where(lanes < B // 2, moved[: B + 8], moved[8:])
        g2m[0:B, 0:B] = moved[:B].astype(BF16)
        g2m[0:B, B : 2 * B] = moved[8:].astype(BF16)
        x_turned = dot_nt(flip[...], x2[B : 2 * B, 0:B]).astype(BF16)
        x_turned = jnp.concatenate([x_turned[B // 2 :], x_turned[: B // 2]], axis=1)
        rows, cols = iotas((B // 2, B))
        keep = cols + rows >= B // 2 - 1
        after = jnp.zeros((B // 2, B), F32)
        for j in reversed(range(blocks // 2)):
            at = slice(16 * j, 16 * j + B)
            pair = dot_nn(x_turned, jnp.concatenate([g2[at, :], g2m[at, :]], axis=0))
            for k, part in ((2 * j + 1, pair[:, B:]), (2 * j, pair[:, :B])):
                mixed = jnp.where(keep, part, after)
                turned = pltpu.roll(mixed, B // 2 + 1, 1, stride=1, stride_axis=0)
                gu[d, :, B * k : B * k + B] = jnp.sum(turned, axis=0, keepdims=True)
                after = part

    @pl.loop(0, 4 * UNITS)
    def _(step):
        u, part = step // 4, step % 4

        @pl.when(part == 0)
        def _():
            gathered(0, u, come)
            unpack(u)

        for d in range(2):
            channel(u, part * 2 + d, d)

        @pl.when(jnp.logical_and(part == 0, u > 0))
        def _():
            send_out(u - 1)

        @pl.when(part == 3)
        def _():
            pack(u)
            hand_out(u)
            send_filter(u)

    last = UNITS - 1
    send_out(last)
    first_ref[...] = g_out[0, :, 0:B]
    for u in range(UNITS):
        gathered(1, u, r_ref)
        rows = pl.ds(UNIT * u, UNIT)
        pltpu.make_async_copy(g_out.at[dp, rows], h_ref.at[dp, rows], g_own.at[u]).wait()
        some = h_ref.at[0:7, rows]
        for sem in (g_send, g_recv):
            wait_for(some, sem.at[u])
        wait_for(going.at[u, :, 2], hand_send.at[0, u])
        wait_for(leaving.at[u, :, 2], hand_send.at[1, u])
        wait_for(come.at[u, 0 : CHIPS - 1], send.at[0, u])
        wait_for(come.at[u, 0 : CHIPS - 1], send.at[1, u])


def exchange(q, k, v, o, filter_taps, skip_gain):
    lags = filter_taps.shape[0]
    share = UNITS * UNIT
    vmem = pl.BlockSpec(memory_space=pltpu.VMEM)
    anywhere = pl.BlockSpec(memory_space=pl.ANY)
    return pl.pallas_call(
        exchange_kernel,
        in_specs=[anywhere] * 5 + [pl.BlockSpec(memory_space=pltpu.SMEM)],
        out_specs=[anywhere, anywhere, vmem],
        out_shape=[
            jax.ShapeDtypeStruct((UNITS, CHIPS, 2, BLOCK, B), BF16),
            jax.ShapeDtypeStruct((8, share, lags // 8), F32),
            jax.ShapeDtypeStruct((share, B), F32),
        ],
        scratch_shapes=[
            *[pltpu.VMEM(q.shape, BF16)] * 4,
            pltpu.VMEM(filter_taps.shape, F32),
            pltpu.VMEM((UNITS, CHIPS, 3, BLOCK, B), BF16),
            pltpu.VMEM((UNITS, CHIPS, 2, BLOCK, B), BF16),
            pltpu.VMEM((UNITS, CHIPS, 3, BLOCK, B), BF16),
            pltpu.VMEM((8, share, lags // 8), F32),
            pltpu.VMEM((share, 1, lags), F32),
            pltpu.VMEM((UNIT * PADDED, B), F32),
            pltpu.VMEM((UNIT * PADDED, B), F32),
            pltpu.VMEM((UNIT * B, B), F32),
            pltpu.VMEM((UNIT * B, B), F32),
            pltpu.VMEM((UNIT, 1, lags), F32),
            pltpu.VMEM((2, 2 * B, 2 * B), BF16),
            pltpu.VMEM((2, 2 * B, 2 * B), BF16),
            pltpu.VMEM((2, 2 * B, 2 * B), BF16),
            pltpu.VMEM((2, lags, B), BF16),
            pltpu.VMEM((2, B, lags), BF16),
            pltpu.VMEM((B, B), BF16),
            pltpu.VMEM((256, 256), BF16),
            pltpu.SemaphoreType.DMA((2, 4)),
            pltpu.SemaphoreType.DMA((2, UNITS)),
            pltpu.SemaphoreType.DMA((2, UNITS)),
            pltpu.SemaphoreType.DMA((2, UNITS)),
            pltpu.SemaphoreType.DMA((2, UNITS)),
            pltpu.SemaphoreType.DMA((2, UNITS)),
            pltpu.SemaphoreType.DMA((UNITS,)),
            pltpu.SemaphoreType.DMA((UNITS,)),
            pltpu.SemaphoreType.DMA((UNITS,)),
            pltpu.SemaphoreType.DMA,
        ],
        compiler_params=pltpu.CompilerParams(
            collective_id=0, has_side_effects=True, vmem_limit_bytes=LIMIT
        ),
        name="exchange",
    )(q, k, v, o, filter_taps, skip_gain)


def finish_kernel(r_ref, k_ref, v_ref, o_ref, h_ref, first_ref, dq_ref, dk_ref, dv_ref, df_ref, ds_ref):
    @pl.when(pl.program_id(0) == 0)
    def _():
        df_ref[...] = jnp.transpose(h_ref[...])
        ds_ref[...] = jnp.transpose(first_ref[...])[0:1]

    rows, cols = iotas((B, B))
    eye = one_hot(rows == cols)
    for m in range(k_ref.shape[1] // 256):
        for half in range(2):
            at = slice(256 * m + 128 * half, 256 * m + 128 * half + 128)
            mixed = r_ref[:, half, :, m // 2, m % 2].astype(F32)
            sorted_rows = jnp.concatenate(
                [
                    mixed[u, dp, which * UNIT : which * UNIT + UNIT]
                    for which in range(2)
                    for dp in range(4)
                    for u in range(UNITS)
                ],
                axis=0,
            ).astype(BF16)
            both = dot_nt(eye, sorted_rows)
            conv, back = both[:, :B], both[:, B:]
            dq_ref[:, at] = (o_ref[:, at].astype(F32) * conv).astype(BF16)
            dk_ref[:, at] = (v_ref[:, at].astype(F32) * back).astype(BF16)
            dv_ref[:, at] = (k_ref[:, at].astype(F32) * back).astype(BF16)


def finish(received, k, v, o, filter_rows, first_lags):
    channels, lags = filter_rows.shape
    width = k.shape[1]
    step = 2048
    spec = pl.BlockSpec((B, step), lambda i: (0, i))
    return pl.pallas_call(
        finish_kernel,
        grid=(width // step,),
        in_specs=[
            pl.BlockSpec(
                (UNITS, 2, 4, step // 512, 2, BLOCK, B),
                lambda i: (0, i * step // 2048, 0, i % (2048 // step), 0, 0, 0),
            )
        ]
        + [spec] * 3
        + [pl.BlockSpec((channels, lags), lambda i: (0, 0)), pl.BlockSpec(first_lags.shape, lambda i: (0, 0))],
        out_specs=[spec] * 3
        + [pl.BlockSpec((lags, channels), lambda i: (0, 0)), pl.BlockSpec((1, first_lags.shape[0]), lambda i: (0, 0))],
        out_shape=[jax.ShapeDtypeStruct((B, width), BF16)] * 3
        + [
            jax.ShapeDtypeStruct((lags, channels), F32),
            jax.ShapeDtypeStruct((1, first_lags.shape[0]), F32),
        ],
        name="finish",
    )(received, k, v, o, filter_rows, first_lags)


def per_device(query_rows, key_rows, value_rows, grad_out, filter_taps, skip_gain):
    q, k, v, o = query_rows[0], key_rows[0], value_rows[0], grad_out[0]
    returned, filter_rows, first_lags = exchange(q, k, v, o, filter_taps, skip_gain)
    returned = returned.reshape(UNITS, 4, 4, 4, 2, BLOCK, B)
    filter_rows = filter_rows.reshape(-1, filter_rows.shape[2])
    dq, dk, dv, d_filter, d_skip = finish(returned, k, v, o, filter_rows, first_lags)
    return dq[None], dk[None], dv[None], d_filter, d_skip[0]


def solution(mesh):
    rows = P("dp", "ctx", None)
    return jax.shard_map(
        per_device,
        mesh=mesh,
        in_specs=(rows, rows, rows, rows, P(None, "ctx"), P("ctx")),
        out_specs=(rows, rows, rows, P("dp", "ctx"), P(("ctx", "dp"))),
        check_vma=False,
    )
```
